768 devices in a mesh: band: 16 (over y, core), field: 48 (over x, z).
Axes of the slice: x: 4, y: 8, z: 12, core: 2. Of those that a mesh axis runs over, the one named last changes fastest.
Arguments:
- spectra: bfloat16 [256, 2, 192, 1280], P('band', None, 'field'), may hold values from -0.29882812 to 0.29882812
- legendre: bfloat16 [256, 128, 1280], P('band'), may hold values from -0.15625 to 0.15625
- wavenum: int32 [256], replicated, may hold values from 0 to 1279, as said below
- dep_row: int32 [128, 4608], P('band', 'field'), may hold values from 0 to 126, as said below
- dep_col: int32 [128, 4608], P('band', 'field'), may hold values from 0 to 4607, as said below
- frac_row: float32 [128, 4608], P('band', 'field'), may hold values from 0 to 1
- frac_col: float32 [128, 4608], P('band', 'field'), may hold values from 0 to 1
Outputs:
- advected: float32 [192, 128, 4608], P(None, 'band', 'field')
The draws below stay inside these ranges and needn't reach their ends.
Inputs may be any that keep to these rules, and one draw needn't show every extreme that they name: `wavenum`: strictly increasing; the first slot holds 0 and the last 1279. `dep_row`: for the arrival point in row r the value lies within r - 2 to r + 1. `dep_col`: for the arrival point in column k the value lies cyclically within k - 2 to k + 1 (mod 4608).
All inputs are finite; a program needn't handle non-finite values.
Results may differ from the reference program's by a relative error of at most 0.0043.
Values may be sent and summed in bfloat16 or wider, within the bound.
No kernel may reach another device: no remote copies, remote signals or barrier semaphores. Data moves between devices by JAX's collectives and lax.ppermute only.
A program may use at most 64 MiB of HBM per device.

```python
import jax
import jax.numpy as jnp
from jax import lax

NN = 1280
NLON = 4608
LATS = 128
HW = 2
MW = 256
FIELDS = 192


def draw_wavenum(key, part):
    inner = jax.random.permutation(key, NN - 2)[:MW - 2].astype(jnp.int32) + 1
    return jnp.concatenate([jnp.zeros((1,), jnp.int32), jnp.sort(inner), jnp.full((1,), NN - 1, jnp.int32)])


def draw_dep_row(key, part):
    rows = lax.broadcasted_iota(jnp.int32, (LATS, NLON), 0)
    offset = jax.random.randint(jax.random.fold_in(key, 11), (LATS, NLON), -HW, HW)
    return jnp.clip(rows + offset, 0, LATS - 2).astype(jnp.int32)


def draw_dep_col(key, part):
    cols = lax.broadcasted_iota(jnp.int32, (LATS, NLON), 1)
    offset = jax.random.randint(jax.random.fold_in(key, 23), (LATS, NLON), -HW, HW)
    return ((cols + offset) % NLON).astype(jnp.int32)


def block_levels(stream_key, dims, split, least, high):
    level, own = 1.0, jax.random.fold_in(stream_key, 6)
    for dim, blocks in split:
        draws = jnp.exp(jax.random.uniform(jax.random.fold_in(own, dim), (blocks,), jnp.float32, least / len(split), high / len(split)))
        level = level * jnp.repeat(draws, dims[dim] // blocks).reshape([-1 if axis == dim else 1 for axis in range(len(dims))])
    return level


def gaussian(key, shape, deviation, bound, split=(), held_as=jnp.bfloat16):
    entries = deviation * jax.random.normal(key, shape, jnp.float32)
    if split:
        entries = entries * block_levels(key, shape, split, -0.22, 0.18)
    return jnp.clip(entries, -bound, bound).astype(held_as)


def setup_inputs(seed: int = 0) -> dict:
    arg_keys = jax.random.split(jax.random.key(seed), 8)
    spectra = gaussian(arg_keys[0], (MW, 2, FIELDS, NN), 0.05, 0.29882812, ((0, 16), (2, 48)))
    legendre = gaussian(arg_keys[1], (MW, LATS, NN), NN ** -0.5, 0.15625, ((0, 16),))
    wavenum = draw_wavenum(jax.random.fold_in(arg_keys[7], 71), 0)
    dep_row = draw_dep_row(jax.random.fold_in(arg_keys[7], 71), 0)
    dep_col = draw_dep_col(jax.random.fold_in(arg_keys[7], 71), 0)
    frac_row = jnp.clip(1.0 * jax.random.uniform(arg_keys[5], (LATS, NLON), jnp.float32) ** block_levels(arg_keys[5], (LATS, NLON), ((0, 16), (1, 48)), -0.2, 0.2), 0.0, 1.0)
    frac_col = jnp.clip(1.0 * jax.random.uniform(arg_keys[6], (LATS, NLON), jnp.float32) ** block_levels(arg_keys[6], (LATS, NLON), ((0, 16), (1, 48)), -0.2, 0.2), 0.0, 1.0)
    return dict(spectra=spectra, legendre=legendre, wavenum=wavenum, dep_row=dep_row, dep_col=dep_col, frac_row=frac_row, frac_col=frac_col)


def fourier_table(wavenum, nlon):
    points = lax.iota(jnp.int32, nlon)
    phase = (wavenum[:, None] * points[None, :]) % nlon
    angle = phase.astype(jnp.float32) * (2.0 * 3.141592653589793 / nlon)
    weight = jnp.where(wavenum == 0, 1.0, 2.0).astype(jnp.float32)[:, None]
    return jnp.stack([weight * jnp.cos(angle), -weight * jnp.sin(angle)], axis=1).astype(jnp.bfloat16)


def reference(spectra, legendre, wavenum, dep_row, dep_col, frac_row, frac_col):
    degree = lax.iota(jnp.int32, NN)

    def one_slot(item):
        spec_slot, table_slot, wave_slot = item
        keep = (degree < (NN - wave_slot)).astype(jnp.float32)
        masked = spec_slot.astype(jnp.float32) * keep[None, None, :]
        return jnp.einsum("cfj,lj->cfl", masked, table_slot.astype(jnp.float32)).astype(jnp.bfloat16)

    four = lax.map(one_slot, (spectra, legendre, wavenum))
    slots = four.shape[0]
    fields = four.shape[2]
    table = fourier_table(wavenum, NLON).reshape(slots * 2, NLON)
    by_field = jnp.moveaxis(four.reshape(slots * 2, fields, LATS), 1, 0)

    def one_field(block):
        return jnp.dot(block.T, table, preferred_element_type=jnp.float32).astype(jnp.bfloat16)

    grid = lax.map(one_field, by_field)
    next_col = (dep_col + 1) % NLON
    upper = dep_row + 1

    def interp(plane):
        plane = plane.astype(jnp.float32)
        low_left = plane[dep_row, dep_col]
        low_right = plane[dep_row, next_col]
        up_left = plane[upper, dep_col]
        up_right = plane[upper, next_col]
        return ((1.0 - frac_row) * (1.0 - frac_col) * low_left + (1.0 - frac_row) * frac_col * low_right
                + frac_row * (1.0 - frac_col) * up_left + frac_row * frac_col * up_right)

    return lax.map(interp, grid)
```

```python
import jax
import jax.numpy as jnp
from jax import lax
from jax.experimental import pallas as pl
from jax.experimental.pallas import tpu as pltpu
from jax.sharding import PartitionSpec as P

NLON = 4608
HW = 2
XS = 4
ZS = 12
J = 3
ZC = ZS // J
PEERS = XS * ZC
TAPS = 2 * HW + 1
WIN = 12
SLAB = 16
LANES = 128
MIB = 1024 * 1024


def legendre_kernel(wave_ref, spec_hbm, leg_hbm, out_ref, spec_buf, leg_buf, pad_ref, spec_sem, leg_sem):
    slots, parts, fields, degrees = spec_buf.shape
    lats = leg_buf.shape[1]
    group = parts * fields
    spec_copy = pltpu.make_async_copy(spec_hbm, spec_buf, spec_sem)
    spec_copy.start()
    leg_copies = [
        pltpu.make_async_copy(leg_hbm.at[s], leg_buf.at[s], leg_sem.at[s]) for s in range(slots)
    ]
    for copy in leg_copies:
        copy.start()
    first = lax.axis_index("band") * slots
    pad_ref[...] = jnp.zeros_like(pad_ref)
    lane_in = lax.broadcasted_iota(jnp.int32, (LANES, LANES), 0)
    lane_out = lax.broadcasted_iota(jnp.int32, (LANES, LANES), 1)
    order = (lane_in % fields) * (LANES // fields) + lane_in // fields
    perm = jnp.where(order == lane_out, 1.0, 0.0).astype(jnp.bfloat16)
    position = lax.broadcasted_iota(jnp.int32, (group, degrees), 1)
    zeros8 = jnp.zeros((group, degrees), jnp.float32)
    spec_copy.wait()
    total = jnp.zeros((lats, LANES), jnp.float32)
    for s in range(slots):
        part = spec_buf[s].astype(jnp.float32)
        rows = jnp.concatenate([part[0], part[1]], axis=0)
        rows = jnp.where(position < degrees - wave_ref[first + s], rows, 0.0)
        pair = [rows, zeros8] if s % 2 == 0 else [zeros8, rows]
        tile = jnp.concatenate(pair, axis=0).astype(jnp.bfloat16)
        pieces = []
        if s // 2 > 0:
            pieces.append(jnp.zeros((2 * group * (s // 2), degrees), jnp.bfloat16))
        pieces.append(tile)
        if s // 2 < slots // 2 - 1:
            pieces.append(
                jnp.zeros((2 * group * (slots // 2 - 1 - s // 2), degrees), jnp.bfloat16)
            )
        weights = jnp.concatenate(pieces, axis=0)
        leg_copies[s].wait()
        total = total + lax.dot_general(
            leg_buf[s], weights, (((1,), (1,)), ((), ())), preferred_element_type=jnp.float32
        )
    four = jnp.dot(total.astype(jnp.bfloat16), perm, preferred_element_type=jnp.float32)
    pad_ref[HW : HW + lats, :] = four
    bands = out_ref.shape[0] // J
    for b in range(bands):
        tile = pad_ref[b * (lats // bands) : b * (lats // bands) + SLAB, :].astype(jnp.bfloat16)
        for j in range(J):
            out_ref[b * J + j] = tile


def reduced_angle(product):
    turns = jnp.floor(product * (1.0 / NLON))
    return (product - turns * NLON) * (2.0 * 3.141592653589793 / NLON)


def table_kernel(wave_ref, start_ref, out_ref):
    rows = out_ref.shape[0]
    wave = wave_ref[...]
    lane = lax.broadcasted_iota(jnp.int32, (rows, LANES), 1).astype(jnp.float32)
    part = (lax.broadcasted_iota(jnp.int32, (rows, LANES), 0) % 2).astype(jnp.float32)
    weight = jnp.where(wave == 0.0, 1.0, 2.0)
    inner = reduced_angle(wave * lane)
    outer = reduced_angle(wave * start_ref[...] + part * (NLON // 4))
    cos_in, sin_in = jnp.cos(inner), jnp.sin(inner)
    cos_out, sin_out = weight * jnp.cos(outer), weight * jnp.sin(outer)
    for p in range(PEERS):
        out_ref[:, p * LANES : (p + 1) * LANES] = (
            cos_out[:, p : p + 1] * cos_in - sin_out[:, p : p + 1] * sin_in
        ).astype(jnp.bfloat16)


def fourier_kernel(four_ref, table_ref, out_ref, flat_ref):
    bands = four_ref.shape[0] // J
    width = 32
    fields = LANES // width
    per_tile = LANES // width
    for j in range(J):
        for q in range(bands // per_tile):
            blocks = [
                four_ref[(per_tile * q + i) * J + j].astype(jnp.float32) for i in range(per_tile)
            ]
            for f in range(fields):
                piece = jnp.concatenate(
                    [block[:WIN, f * width : (f + 1) * width] for block in blocks], axis=1
                )
                row = (j * fields + f) * WIN
                flat_ref[row : row + WIN, q * LANES : (q + 1) * LANES] = piece
    flat = flat_ref[...].astype(jnp.bfloat16)
    for n in range(PEERS // 2):
        grid = jnp.dot(
            flat,
            table_ref[:, 2 * n * LANES : 2 * (n + 1) * LANES],
            preferred_element_type=jnp.float32,
        ).astype(jnp.bfloat16)
        out_ref[2 * n] = grid[:, :LANES]
        out_ref[2 * n + 1] = grid[:, LANES:]


def interp_kernel(grid_ref, dep_row, dep_col, frac_row, frac_col, out_ref, buf, weight_ref):
    rows, cols = dep_row.shape
    fields = 4
    row_ids = lax.axis_index("band") * rows + lax.broadcasted_iota(jnp.int32, (rows, cols), 0)
    col_ids = lax.axis_index("field") * cols + lax.broadcasted_iota(jnp.int32, (rows, cols), 1)
    delta_row = dep_row[...] - row_ids
    delta_col = dep_col[...] - col_ids + HW
    delta_col = jnp.where(delta_col < 0, delta_col + NLON, delta_col)
    delta_col = jnp.where(delta_col >= NLON, delta_col - NLON, delta_col) - HW
    a = frac_row[...]
    b = frac_col[...]

    def hats(delta, frac):
        return [
            jnp.where(delta == o, 1.0 - frac, 0.0) + jnp.where(delta + 1 == o, frac, 0.0)
            for o in range(-HW, HW + 1)
        ]

    row_hats, col_hats = hats(delta_row, a), hats(delta_col, b)
    weight_ref[...] = jnp.zeros_like(weight_ref)
    for d in range(TAPS):
        for e in range(TAPS):
            weight_ref[d * TAPS + e, :, :cols] = row_hats[d] * col_hats[e]
    taps = [
        pltpu.roll(weight_ref[d * TAPS + e], e, 1) if e else weight_ref[d * TAPS]
        for d in range(TAPS)
        for e in range(TAPS)
    ]
    depth = grid_ref.shape[1]
    for p in range(PEERS):
        buf[p * depth : (p + 1) * depth, :] = grid_ref[p].astype(jnp.float32)

    def body(i, carry):
        p, j = i // J, i % J
        z = p % ZC + ZC * j
        field = ((p // ZC) * ZS + z) * fields
        for f in range(fields):
            base = i * (fields * WIN) + f * WIN
            planes = [buf[pl.ds(base + d, rows), :] for d in range(TAPS)]
            result = None
            for e in range(TAPS):
                column = planes[0] * taps[e]
                for d in range(1, TAPS):
                    column = column + planes[d] * taps[d * TAPS + e]
                column = pltpu.roll(column, LANES - e, 1) if e else column
                result = column if result is None else result + column
            out_ref[field + f] = result[:, :cols]
        return carry

    lax.fori_loop(0, PEERS * J, body, 0)


def exchange_groups(bands):
    first, second = [], []
    for x in range(XS):
        for i in range(ZC):
            first.append(
                [b * XS * ZS + x * ZS + i + ZC * j for b in range(bands) for j in range(J)]
            )
    for b in range(bands):
        shift = ZC // 2 if b % 2 and J > 1 else 0
        for g in range(J):
            window = sorted(((ZC * g + shift + n) % ZS for n in range(ZC)), key=lambda z: z % ZC)
            second.append([b * XS * ZS + x * ZS + z for x in range(XS) for z in window])
    return first, second


def local(spectra, legendre, wavenum, dep_row, dep_col, frac_row, frac_col):
    bands = lax.axis_size("band")
    band = lax.axis_index("band")
    field = lax.axis_index("field")
    slots, parts, fields, degrees = spectra.shape
    lats = legendre.shape[1]
    waves = wavenum.shape[0]
    rows, cols = dep_row.shape
    first, second = exchange_groups(bands)
    vmem = pl.BlockSpec(memory_space=pltpu.VMEM)
    hbm = pl.BlockSpec(memory_space=pltpu.HBM)
    smem = pl.BlockSpec(memory_space=pltpu.SMEM)

    four = pl.pallas_call(
        legendre_kernel,
        out_shape=jax.ShapeDtypeStruct((bands * J, SLAB, LANES), jnp.bfloat16),
        in_specs=[smem, hbm, hbm],
        out_specs=vmem,
        scratch_shapes=[
            pltpu.VMEM(spectra.shape, jnp.bfloat16),
            pltpu.VMEM(legendre.shape, jnp.bfloat16),
            pltpu.VMEM((lats + SLAB, LANES), jnp.float32),
            pltpu.SemaphoreType.DMA,
            pltpu.SemaphoreType.DMA((slots,)),
        ],
        compiler_params=pltpu.CompilerParams(vmem_limit_bytes=24 * MIB),
        cost_estimate=pl.CostEstimate(
            flops=2 * slots * LANES * lats * degrees, bytes_accessed=6 * MIB, transcendentals=0
        ),
        name="legendre",
    )(wavenum, spectra, legendre)
    rows_here = lax.all_to_all(
        four, ("band", "field"), split_axis=0, concat_axis=0, tiled=True, axis_index_groups=first
    )

    z_here = field % ZS
    mod_here = z_here % ZC
    shift = jnp.where(band % 2 == 1, ZC // 2 if J > 1 else 0, 0)
    group = (z_here // ZC - jnp.where(mod_here < shift, 1, 0)) % J
    peer = jnp.minimum(lax.iota(jnp.int32, LANES), PEERS - 1)
    mod_peer = peer % ZC
    z_peer = (ZC * group + mod_peer + jnp.where(mod_peer < shift, ZC, 0)) % ZS
    start = ((peer // ZC) * ZS + z_peer) * cols - HW
    start = jnp.where(start < 0, start + NLON, start)
    wave_rows = jnp.broadcast_to(wavenum[:, None], (waves, parts)).reshape(waves * parts, 1)
    table = pl.pallas_call(
        table_kernel,
        out_shape=jax.ShapeDtypeStruct((waves * parts, PEERS * LANES), jnp.bfloat16),
        in_specs=[vmem, vmem],
        out_specs=vmem,
        compiler_params=pltpu.CompilerParams(vmem_limit_bytes=24 * MIB),
        cost_estimate=pl.CostEstimate(
            flops=20 * MIB, bytes_accessed=4 * MIB, transcendentals=MIB // 4
        ),
        name="table",
    )(wave_rows.astype(jnp.float32), start.astype(jnp.float32)[None, :])

    depth = J * fields * WIN
    grid = pl.pallas_call(
        fourier_kernel,
        out_shape=jax.ShapeDtypeStruct((PEERS, depth, LANES), jnp.bfloat16),
        in_specs=[vmem, vmem],
        out_specs=vmem,
        scratch_shapes=[pltpu.VMEM((depth, waves * parts), jnp.float32)],
        compiler_params=pltpu.CompilerParams(vmem_limit_bytes=24 * MIB),
        cost_estimate=pl.CostEstimate(
            flops=2 * depth * waves * parts * PEERS * LANES,
            bytes_accessed=3 * MIB,
            transcendentals=0,
        ),
        name="fourier",
    )(rows_here, table)
    segment = lax.all_to_all(
        grid, ("band", "field"), split_axis=0, concat_axis=0, tiled=True, axis_index_groups=second
    )
    total_fields = XS * ZS * fields
    return pl.pallas_call(
        interp_kernel,
        out_shape=jax.ShapeDtypeStruct((total_fields, rows, cols), jnp.float32),
        in_specs=[vmem] * 5,
        out_specs=vmem,
        scratch_shapes=[
            pltpu.VMEM((PEERS * depth, LANES), jnp.float32),
            pltpu.VMEM((TAPS * TAPS, rows, LANES), jnp.float32),
        ],
        compiler_params=pltpu.CompilerParams(vmem_limit_bytes=24 * MIB),
        cost_estimate=pl.CostEstimate(
            flops=50 * total_fields * rows * LANES, bytes_accessed=2 * MIB, transcendentals=0
        ),
        name="interp",
    )(segment, dep_row, dep_col, frac_row, frac_col)


def solution(mesh):
    return jax.shard_map(
        local,
        mesh=mesh,
        in_specs=(
            P("band", None, "field", None),
            P("band", None, None),
            P(),
            P("band", "field"),
            P("band", "field"),
            P("band", "field"),
            P("band", "field"),
        ),
        out_specs=P(None, "band", "field"),
        check_vma=False,
    )
```

```python
import jax
import jax.numpy as jnp
from jax import lax
from jax.experimental import pallas as pl
from jax.experimental.pallas import tpu as pltpu
from jax.sharding import PartitionSpec as P

NLON = 4608
HW = 2
XS = 4
ZS = 12
J = 3
ZC = ZS // J
PEERS = XS * ZC
TAPS = 2 * HW + 1
WIN = 12
SLAB = 16
CHUNKS = 1
LANES = 128
MIB = 1024 * 1024


def legendre_kernel(
    wave_hbm, spec_hbm, leg_hbm, out_ref, wave_ref, spec_buf, leg_buf, pad_ref, small_sem, leg_sem
):
    slots, parts, fields, degrees = spec_buf.shape
    lats = leg_buf.shape[1]
    group = parts * fields
    chunks = leg_sem.shape[0]
    per_chunk = slots // chunks
    wave_copy = pltpu.make_async_copy(wave_hbm, wave_ref, small_sem.at[0])
    spec_copy = pltpu.make_async_copy(spec_hbm, spec_buf, small_sem.at[1])
    spec_copy.start()
    wave_copy.start()
    leg_copies = []
    for c in range(chunks):
        part = pl.ds(c * per_chunk, per_chunk)
        leg_copies.append(
            pltpu.make_async_copy(leg_hbm.at[part], leg_buf.at[part], leg_sem.at[c])
        )
    for copy in leg_copies:
        copy.start()
    first = lax.axis_index("band") * slots
    pad_ref[:8, :] = jnp.zeros((8, LANES), jnp.float32)
    pad_ref[lats:, :] = jnp.zeros((SLAB, LANES), jnp.float32)
    lane_in = lax.broadcasted_iota(jnp.int32, (LANES, LANES), 0)
    lane_out = lax.broadcasted_iota(jnp.int32, (LANES, LANES), 1)
    order = (lane_in % fields) * (LANES // fields) + lane_in // fields
    perm = jnp.where(order == lane_out, 1.0, 0.0).astype(jnp.bfloat16)
    position = lax.broadcasted_iota(jnp.int32, (group, degrees), 1)
    slot_of_lane = lax.broadcasted_iota(jnp.int32, (lats, LANES), 1) // group
    wave_copy.wait()
    spec_copy.wait()
    kept = []
    for s in range(slots):
        part = spec_buf[s].astype(jnp.float32)
        rows = jnp.concatenate([part[0], part[1]], axis=0)
        kept.append(jnp.where(position < degrees - wave_ref[first + s], rows, 0.0))
    weights = jnp.concatenate(kept, axis=0).astype(jnp.bfloat16)
    total = jnp.zeros((lats, LANES), jnp.float32)
    for c in range(chunks):
        leg_copies[c].wait()
        rows = leg_buf[c * per_chunk : (c + 1) * per_chunk].reshape(per_chunk * lats, degrees)
        products = lax.dot_general(
            rows, weights, (((1,), (1,)), ((), ())), preferred_element_type=jnp.float32
        )
        for n in range(per_chunk):
            own = slot_of_lane == c * per_chunk + n
            total = jnp.where(own, products[n * lats : (n + 1) * lats], total)
    four = jnp.dot(total.astype(jnp.bfloat16), perm, preferred_element_type=jnp.float32)
    pad_ref[HW : HW + lats, :] = four
    bands = out_ref.shape[0] // J
    for b in range(bands):
        tile = pad_ref[b * (lats // bands) : b * (lats // bands) + SLAB, :].astype(jnp.bfloat16)
        for j in range(J):
            out_ref[b * J + j] = tile


def reduced_angle(product):
    turns = jnp.floor(product * (1.0 / NLON))
    return (product - turns * NLON) * (2.0 * 3.141592653589793 / NLON)


def table_kernel(wave_ref, start_ref, out_ref):
    rows = out_ref.shape[0]
    wave = wave_ref[...]
    lane = lax.broadcasted_iota(jnp.int32, (rows, LANES), 1).astype(jnp.float32)
    part = (lax.broadcasted_iota(jnp.int32, (rows, LANES), 0) % 2).astype(jnp.float32)
    weight = jnp.where(wave == 0.0, 1.0, 2.0)
    inner = reduced_angle(wave * lane)
    outer = reduced_angle(wave * start_ref[...] + part * (NLON // 4))
    cos_in, sin_in = jnp.cos(inner), jnp.sin(inner)
    cos_out, sin_out = weight * jnp.cos(outer), weight * jnp.sin(outer)
    for p in range(PEERS):
        out_ref[:, p * LANES : (p + 1) * LANES] = (
            cos_out[:, p : p + 1] * cos_in - sin_out[:, p : p + 1] * sin_in
        ).astype(jnp.bfloat16)


def fourier_kernel(four_ref, table_ref, out_ref, flat_ref):
    bands = four_ref.shape[0] // J
    width = 32
    fields = LANES // width
    per_tile = LANES // width
    for j in range(J):
        for q in range(bands // per_tile):
            blocks = [
                four_ref[(per_tile * q + i) * J + j].astype(jnp.float32) for i in range(per_tile)
            ]
            for f in range(fields):
                piece = jnp.concatenate(
                    [block[:WIN, f * width : (f + 1) * width] for block in blocks], axis=1
                )
                row = (j * fields + f) * WIN
                flat_ref[row : row + WIN, q * LANES : (q + 1) * LANES] = piece
    flat = flat_ref[...].astype(jnp.bfloat16)
    for n in range(PEERS // 2):
        grid = jnp.dot(
            flat,
            table_ref[:, 2 * n * LANES : 2 * (n + 1) * LANES],
            preferred_element_type=jnp.float32,
        ).astype(jnp.bfloat16)
        out_ref[2 * n] = grid[:, :LANES]
        out_ref[2 * n + 1] = grid[:, LANES:]


def interp_kernel(grid_ref, dep_row, dep_col, frac_row, frac_col, out_ref, buf, weight_ref):
    rows, cols = dep_row.shape
    fields = 4
    row_ids = lax.axis_index("band") * rows + lax.broadcasted_iota(jnp.int32, (rows, cols), 0)
    col_ids = lax.axis_index("field") * cols + lax.broadcasted_iota(jnp.int32, (rows, cols), 1)
    delta_row = dep_row[...] - row_ids
    delta_col = dep_col[...] - col_ids + HW
    delta_col = jnp.where(delta_col < 0, delta_col + NLON, delta_col)
    delta_col = jnp.where(delta_col >= NLON, delta_col - NLON, delta_col) - HW
    a = frac_row[...]
    b = frac_col[...]

    def hats(delta, frac):
        return [
            jnp.where(delta == o, 1.0 - frac, 0.0) + jnp.where(delta + 1 == o, frac, 0.0)
            for o in range(-HW, HW + 1)
        ]

    row_hats, col_hats = hats(delta_row, a), hats(delta_col, b)
    weight_ref[...] = jnp.zeros_like(weight_ref)
    for d in range(TAPS):
        for e in range(TAPS):
            weight_ref[d * TAPS + e, :, :cols] = row_hats[d] * col_hats[e]
    taps = [
        pltpu.roll(weight_ref[d * TAPS + e], e, 1) if e else weight_ref[d * TAPS]
        for d in range(TAPS)
        for e in range(TAPS)
    ]
    depth = grid_ref.shape[1]
    for p in range(PEERS):
        buf[p * depth : (p + 1) * depth, :] = grid_ref[p].astype(jnp.float32)

    def body(p, carry):
        for t in range(J * fields):
            base = pl.multiple_of(p * depth, 8) + t * WIN
            planes = [buf[pl.ds(base + d, rows), :] for d in range(TAPS)]
            result = None
            for e in range(TAPS):
                column = planes[0] * taps[e]
                for d in range(1, TAPS):
                    column = column + planes[d] * taps[d * TAPS + e]
                column = pltpu.roll(column, LANES - e, 1) if e else column
                result = column if result is None else result + column
            z = p // XS + ZC * (t // fields)
            out_ref[((p % XS) * ZS + z) * fields + t % fields] = result[:, :cols]
        return carry

    lax.fori_loop(0, PEERS, body, 0)


def exchange_groups(bands):
    first, second = [], []
    for x in range(XS):
        for i in range(ZC):
            first.append(
                [b * XS * ZS + x * ZS + i + ZC * j for b in range(bands) for j in range(J)]
            )
    for b in range(bands):
        shift = ZC // 2 if b % 2 and J > 1 else 0
        for g in range(J):
            window = sorted(((ZC * g + shift + n) % ZS for n in range(ZC)), key=lambda z: z % ZC)
            second.append([b * XS * ZS + x * ZS + z for z in window for x in range(XS)])
    return first, second


def local(spectra, legendre, wavenum, dep_row, dep_col, frac_row, frac_col):
    bands = lax.axis_size("band")
    band = lax.axis_index("band")
    field = lax.axis_index("field")
    slots, parts, fields, degrees = spectra.shape
    lats = legendre.shape[1]
    waves = wavenum.shape[0]
    rows, cols = dep_row.shape
    first, second = exchange_groups(bands)
    vmem = pl.BlockSpec(memory_space=pltpu.VMEM)
    hbm = pl.BlockSpec(memory_space=pltpu.HBM)

    four = pl.pallas_call(
        legendre_kernel,
        out_shape=jax.ShapeDtypeStruct((bands * J, SLAB, LANES), jnp.bfloat16),
        in_specs=[hbm, hbm, hbm],
        out_specs=vmem,
        scratch_shapes=[
            pltpu.SMEM(wavenum.shape, jnp.int32),
            pltpu.VMEM(spectra.shape, jnp.bfloat16),
            pltpu.VMEM(legendre.shape, jnp.bfloat16),
            pltpu.VMEM((lats + SLAB, LANES), jnp.float32),
            pltpu.SemaphoreType.DMA((2,)),
            pltpu.SemaphoreType.DMA((CHUNKS,)),
        ],
        compiler_params=pltpu.CompilerParams(vmem_limit_bytes=60 * MIB),
        cost_estimate=pl.CostEstimate(
            flops=2 * slots * LANES * lats * degrees, bytes_accessed=6 * MIB, transcendentals=0
        ),
        name="legendre",
    )(wavenum, spectra, legendre)
    rows_here = lax.all_to_all(
        four, ("band", "field"), split_axis=0, concat_axis=0, tiled=True, axis_index_groups=first
    )

    z_here = field % ZS
    mod_here = z_here % ZC
    shift = jnp.where(band % 2 == 1, ZC // 2 if J > 1 else 0, 0)
    group = (z_here // ZC - jnp.where(mod_here < shift, 1, 0)) % J
    peer = jnp.minimum(lax.iota(jnp.int32, LANES), PEERS - 1)
    mod_peer = peer // XS
    z_peer = (ZC * group + mod_peer + jnp.where(mod_peer < shift, ZC, 0)) % ZS
    start = ((peer % XS) * ZS + z_peer) * cols - HW
    start = jnp.where(start < 0, start + NLON, start)
    wave_rows = jnp.broadcast_to(wavenum[:, None], (waves, parts)).reshape(waves * parts, 1)
    table = pl.pallas_call(
        table_kernel,
        out_shape=jax.ShapeDtypeStruct((waves * parts, PEERS * LANES), jnp.bfloat16),
        in_specs=[vmem, vmem],
        out_specs=vmem,
        compiler_params=pltpu.CompilerParams(vmem_limit_bytes=24 * MIB),
        cost_estimate=pl.CostEstimate(
            flops=20 * MIB, bytes_accessed=4 * MIB, transcendentals=MIB // 4
        ),
        name="table",
    )(wave_rows.astype(jnp.float32), start.astype(jnp.float32)[None, :])

    depth = J * fields * WIN
    grid = pl.pallas_call(
        fourier_kernel,
        out_shape=jax.ShapeDtypeStruct((PEERS, depth, LANES), jnp.bfloat16),
        in_specs=[vmem, vmem],
        out_specs=vmem,
        scratch_shapes=[pltpu.VMEM((depth, waves * parts), jnp.float32)],
        compiler_params=pltpu.CompilerParams(vmem_limit_bytes=24 * MIB),
        cost_estimate=pl.CostEstimate(
            flops=2 * depth * waves * parts * PEERS * LANES,
            bytes_accessed=3 * MIB,
            transcendentals=0,
        ),
        name="fourier",
    )(rows_here, table)
    segment = lax.all_to_all(
        grid, ("band", "field"), split_axis=0, concat_axis=0, tiled=True, axis_index_groups=second
    )
    total_fields = XS * ZS * fields
    return pl.pallas_call(
        interp_kernel,
        out_shape=jax.ShapeDtypeStruct((total_fields, rows, cols), jnp.float32),
        in_specs=[vmem] * 5,
        out_specs=vmem,
        scratch_shapes=[
            pltpu.VMEM((PEERS * depth, LANES), jnp.float32),
            pltpu.VMEM((TAPS * TAPS, rows, LANES), jnp.float32),
        ],
        compiler_params=pltpu.CompilerParams(vmem_limit_bytes=24 * MIB),
        cost_estimate=pl.CostEstimate(
            flops=50 * total_fields * rows * LANES, bytes_accessed=2 * MIB, transcendentals=0
        ),
        name="interp",
    )(segment, dep_row, dep_col, frac_row, frac_col)


def solution(mesh):
    return jax.shard_map(
        local,
        mesh=mesh,
        in_specs=(
            P("band", None, "field", None),
            P("band", None, None),
            P(),
            P("band", "field"),
            P("band", "field"),
            P("band", "field"),
            P("band", "field"),
        ),
        out_specs=P(None, "band", "field"),
        check_vma=False,
    )
```

```python
import jax
import jax.numpy as jnp
from jax import lax
from jax.experimental import pallas as pl
from jax.experimental.pallas import tpu as pltpu
from jax.sharding import PartitionSpec as P

NLON = 4608
HW = 2
XS = 4
ZS = 12
J = 3
ZC = ZS // J
PEERS = XS * ZC
TAPS = 2 * HW + 1
WIN = 12
SLAB = 16
CHUNKS = 1
WIDE = 64
SPLIT = WIDE - 2 * HW
THIN = 40
LANES = 128
MIB = 1024 * 1024


def legendre_kernel(
    wave_hbm, spec_hbm, leg_hbm, out_ref, wave_ref, spec_buf, leg_buf, pad_ref, small_sem, leg_sem
):
    slots, parts, fields, degrees = spec_buf.shape
    lats = leg_buf.shape[1]
    group = parts * fields
    chunks = leg_sem.shape[0]
    per_chunk = slots // chunks
    wave_copy = pltpu.make_async_copy(wave_hbm, wave_ref, small_sem.at[0])
    spec_copy = pltpu.make_async_copy(spec_hbm, spec_buf, small_sem.at[1])
    spec_copy.start()
    wave_copy.start()
    leg_copies = []
    for c in range(chunks):
        part = pl.ds(c * per_chunk, per_chunk)
        leg_copies.append(
            pltpu.make_async_copy(leg_hbm.at[part], leg_buf.at[part], leg_sem.at[c])
        )
    for copy in leg_copies:
        copy.start()
    first = lax.axis_index("band") * slots
    pad_ref[:8, :] = jnp.zeros((8, LANES), jnp.float32)
    pad_ref[lats:, :] = jnp.zeros((SLAB, LANES), jnp.float32)
    lane_in = lax.broadcasted_iota(jnp.int32, (LANES, LANES), 0)
    lane_out = lax.broadcasted_iota(jnp.int32, (LANES, LANES), 1)
    order = (lane_in % fields) * (LANES // fields) + lane_in // fields
    perm = jnp.where(order == lane_out, 1.0, 0.0).astype(jnp.bfloat16)
    position = lax.broadcasted_iota(jnp.int32, (group, degrees), 1)
    slot_of_lane = lax.broadcasted_iota(jnp.int32, (lats, LANES), 1) // group
    wave_copy.wait()
    spec_copy.wait()
    kept = []
    for s in range(slots):
        part = spec_buf[s].astype(jnp.float32)
        rows = jnp.concatenate([part[0], part[1]], axis=0)
        kept.append(jnp.where(position < degrees - wave_ref[first + s], rows, 0.0))
    weights = jnp.concatenate(kept, axis=0).astype(jnp.bfloat16)
    total = jnp.zeros((lats, LANES), jnp.float32)
    for c in range(chunks):
        leg_copies[c].wait()
        rows = leg_buf[c * per_chunk : (c + 1) * per_chunk].reshape(per_chunk * lats, degrees)
        products = lax.dot_general(
            rows, weights, (((1,), (1,)), ((), ())), preferred_element_type=jnp.float32
        )
        for n in range(per_chunk):
            own = slot_of_lane == c * per_chunk + n
            total = jnp.where(own, products[n * lats : (n + 1) * lats], total)
    four = jnp.dot(total.astype(jnp.bfloat16), perm, preferred_element_type=jnp.float32)
    pad_ref[HW : HW + lats, :] = four
    bands = out_ref.shape[0] // J
    for b in range(bands):
        tile = pad_ref[b * (lats // bands) : b * (lats // bands) + SLAB, :].astype(jnp.bfloat16)
        for j in range(J):
            out_ref[b * J + j] = tile


def turn_parts(product):
    quarters = product * (4.0 / NLON)
    nearest = jnp.floor(quarters + 0.5)
    x = (product - nearest * (NLON / 4)) * (2.0 * 3.141592653589793 / NLON)
    square = x * x
    sine = x * (1.0 + square * (-1.0 / 6 + square * (1.0 / 120 + square * (-1.0 / 5040 + square * (1.0 / 362880)))))
    cosine = 1.0 + square * (
        -0.5 + square * (1.0 / 24 + square * (-1.0 / 720 + square * (1.0 / 40320 - square * (1.0 / 3628800))))
    )
    quadrant = nearest.astype(jnp.int32)
    swap = (quadrant & 1) == 1
    cos_value = jnp.where(swap, sine, cosine)
    sin_value = jnp.where(swap, cosine, sine)
    cos_value = jnp.where(((quadrant + 1) & 2) == 2, -cos_value, cos_value)
    sin_value = jnp.where((quadrant & 2) == 2, -sin_value, sin_value)
    return cos_value, sin_value


def table_kernel(wave_ref, start_ref, out_ref):
    rows = out_ref.shape[0]
    wave = wave_ref[...]
    lane = lax.broadcasted_iota(jnp.int32, (rows, LANES), 1)
    part = (lax.broadcasted_iota(jnp.int32, (rows, LANES), 0) % 2).astype(jnp.float32)
    weight = jnp.where(wave == 0.0, 1.0, 2.0)
    column_a = lane & (WIDE - 1)
    column_b = jnp.where(lane < THIN, lane, jnp.where(lane < 2 * THIN, lane - THIN, lane - 2 * THIN))
    column_b = column_b + SPLIT
    inner = [turn_parts(wave * column.astype(jnp.float32)) for column in (column_a, column_b)]
    cos_out, sin_out = turn_parts(wave * start_ref[...] + part * (NLON // 4))
    cos_out, sin_out = weight * cos_out, weight * sin_out
    for p in range(PEERS):
        cos_p, sin_p = cos_out[:, p : p + 1], sin_out[:, p : p + 1]
        for n, (cos_in, sin_in) in enumerate(inner):
            first = (2 * p + n) * LANES
            out_ref[:, first : first + LANES] = (cos_p * cos_in - sin_p * sin_in).astype(jnp.bfloat16)


def fourier_kernel(four_ref, table_ref, out_ref, flat_ref):
    bands = four_ref.shape[0] // J
    width = 32
    fields = LANES // width
    per_tile = LANES // width
    for j in range(J):
        for q in range(bands // per_tile):
            blocks = [
                four_ref[(per_tile * q + i) * J + j].astype(jnp.float32) for i in range(per_tile)
            ]
            for f in range(fields):
                piece = jnp.concatenate(
                    [block[:WIN, f * width : (f + 1) * width] for block in blocks], axis=1
                )
                row = (j * fields + f) * WIN
                flat_ref[row : row + WIN, q * LANES : (q + 1) * LANES] = piece
    flat = flat_ref[...].astype(jnp.bfloat16)
    depth = flat.shape[0]
    half, third = depth // 2, depth // 3
    in_low = lax.broadcasted_iota(jnp.int32, (half, LANES), 1) < WIDE
    lane = lax.broadcasted_iota(jnp.int32, (third, LANES), 1)
    for p in range(PEERS):
        both = jnp.dot(
            flat,
            table_ref[:, 2 * p * LANES : 2 * (p + 1) * LANES],
            preferred_element_type=jnp.float32,
        )
        wide, thin = both[:, :LANES], both[:, LANES:]
        wide = jnp.where(in_low, wide[:half], wide[half:])
        thin = jnp.where(
            lane < THIN,
            thin[:third],
            jnp.where(lane < 2 * THIN, thin[third : 2 * third], thin[2 * third :]),
        )
        out_ref[p] = jnp.concatenate([wide, thin], axis=0).astype(jnp.bfloat16)


def interp_kernel(grid_ref, dep_row, dep_col, frac_row, frac_col, out_ref, buf, weight_ref):
    rows, cols = dep_row.shape
    fields = 4
    row_ids = lax.axis_index("band") * rows + lax.broadcasted_iota(jnp.int32, (rows, cols), 0)
    col_ids = lax.axis_index("field") * cols + lax.broadcasted_iota(jnp.int32, (rows, cols), 1)
    delta_row = dep_row[...] - row_ids
    delta_col = dep_col[...] - col_ids + HW
    delta_col = jnp.where(delta_col < 0, delta_col + NLON, delta_col)
    delta_col = jnp.where(delta_col >= NLON, delta_col - NLON, delta_col) - HW
    a = frac_row[...]
    b = frac_col[...]

    def hats(delta, frac):
        return [
            jnp.where(delta == o, 1.0 - frac, 0.0) + jnp.where(delta + 1 == o, frac, 0.0)
            for o in range(-HW, HW + 1)
        ]

    row_hats, col_hats = hats(delta_row, a), hats(delta_col, b)
    scratch = weight_ref.shape[0] - 1
    weight_ref[scratch] = jnp.zeros((rows, LANES), jnp.float32)
    lane = lax.broadcasted_iota(jnp.int32, (rows, LANES), 1)
    for d in range(TAPS):
        for e in range(TAPS):
            weight_ref[scratch, :, :cols] = row_hats[d] * col_hats[e]
            tap = weight_ref[scratch]
            wide = jnp.where(lane < SPLIT, tap, 0.0)
            thin = pltpu.roll(jnp.where(lane < SPLIT, 0.0, tap), LANES - SPLIT, 1)
            wide = wide + pltpu.roll(wide, WIDE, 1)
            thin = thin + pltpu.roll(thin, THIN, 1) + pltpu.roll(thin, 2 * THIN, 1)
            weight_ref[d * TAPS + e] = pltpu.roll(wide, e, 1) if e else wide
            weight_ref[TAPS * TAPS + d * TAPS + e] = pltpu.roll(thin, e, 1) if e else thin
    depth = grid_ref.shape[1]
    per_peer = J * fields
    for p in range(PEERS):
        buf[p * depth : (p + 1) * depth, :] = grid_ref[p].astype(jnp.float32)

    def stencil(base, first_tap):
        planes = [buf[pl.ds(base + d, rows), :] for d in range(TAPS)]
        result = None
        for e in range(TAPS):
            column = planes[0] * weight_ref[first_tap + e]
            for d in range(1, TAPS):
                column = column + planes[d] * weight_ref[first_tap + d * TAPS + e]
            column = pltpu.roll(column, LANES - e, 1) if e else column
            result = column if result is None else result + column
        return result

    def body(p, carry):
        base = pl.multiple_of(p * depth, 8)
        wide = [stencil(base + u * WIN, 0) for u in range(per_peer // 2)]
        low = base + (per_peer // 2) * WIN
        thin = [stencil(low + v * WIN, TAPS * TAPS) for v in range(per_peer // 3)]
        for t in range(per_peer):
            left = wide[t % (per_peer // 2)]
            left = pltpu.roll(left, WIDE, 1) if t >= per_peer // 2 else left
            right = thin[t % (per_peer // 3)]
            right = pltpu.roll(right, (SPLIT - THIN * (t // (per_peer // 3))) % LANES, 1)
            z = p // XS + ZC * (t // fields)
            row = ((p % XS) * ZS + z) * fields + t % fields
            out_ref[row] = jnp.where(lane < SPLIT, left, right)[:, :cols]
        return carry

    lax.fori_loop(0, PEERS, body, 0)


def exchange_groups(bands):
    first, second = [], []
    for x in range(XS):
        for i in range(ZC):
            first.append(
                [b * XS * ZS + x * ZS + i + ZC * j for b in range(bands) for j in range(J)]
            )
    for b in range(bands):
        shift = ZC // 2 if b % 2 and J > 1 else 0
        for g in range(J):
            window = sorted(((ZC * g + shift + n) % ZS for n in range(ZC)), key=lambda z: z % ZC)
            second.append([b * XS * ZS + x * ZS + z for z in window for x in range(XS)])
    return first, second


def local(spectra, legendre, wavenum, dep_row, dep_col, frac_row, frac_col):
    bands = lax.axis_size("band")
    band = lax.axis_index("band")
    field = lax.axis_index("field")
    slots, parts, fields, degrees = spectra.shape
    lats = legendre.shape[1]
    waves = wavenum.shape[0]
    rows, cols = dep_row.shape
    first, second = exchange_groups(bands)
    vmem = pl.BlockSpec(memory_space=pltpu.VMEM)
    hbm = pl.BlockSpec(memory_space=pltpu.HBM)

    four = pl.pallas_call(
        legendre_kernel,
        out_shape=jax.ShapeDtypeStruct((bands * J, SLAB, LANES), jnp.bfloat16),
        in_specs=[hbm, hbm, hbm],
        out_specs=vmem,
        scratch_shapes=[
            pltpu.SMEM(wavenum.shape, jnp.int32),
            pltpu.VMEM(spectra.shape, jnp.bfloat16),
            pltpu.VMEM(legendre.shape, jnp.bfloat16),
            pltpu.VMEM((lats + SLAB, LANES), jnp.float32),
            pltpu.SemaphoreType.DMA((2,)),
            pltpu.SemaphoreType.DMA((CHUNKS,)),
        ],
        compiler_params=pltpu.CompilerParams(vmem_limit_bytes=60 * MIB),
        cost_estimate=pl.CostEstimate(
            flops=2 * slots * LANES * lats * degrees, bytes_accessed=6 * MIB, transcendentals=0
        ),
        name="legendre",
    )(wavenum, spectra, legendre)
    rows_here = lax.all_to_all(
        four, ("band", "field"), split_axis=0, concat_axis=0, tiled=True, axis_index_groups=first
    )

    z_here = field % ZS
    mod_here = z_here % ZC
    shift = jnp.where(band % 2 == 1, ZC // 2 if J > 1 else 0, 0)
    group = (z_here // ZC - jnp.where(mod_here < shift, 1, 0)) % J
    peer = jnp.minimum(lax.iota(jnp.int32, LANES), PEERS - 1)
    mod_peer = peer // XS
    z_peer = (ZC * group + mod_peer + jnp.where(mod_peer < shift, ZC, 0)) % ZS
    start = ((peer % XS) * ZS + z_peer) * cols - HW
    start = jnp.where(start < 0, start + NLON, start)
    wave_rows = jnp.broadcast_to(wavenum[:, None], (waves, parts)).reshape(waves * parts, 1)
    table = pl.pallas_call(
        table_kernel,
        out_shape=jax.ShapeDtypeStruct((waves * parts, 2 * PEERS * LANES), jnp.bfloat16),
        in_specs=[vmem, vmem],
        out_specs=vmem,
        compiler_params=pltpu.CompilerParams(vmem_limit_bytes=24 * MIB),
        cost_estimate=pl.CostEstimate(
            flops=20 * MIB, bytes_accessed=4 * MIB, transcendentals=MIB // 4
        ),
        name="table",
    )(wave_rows.astype(jnp.float32), start.astype(jnp.float32)[None, :])

    depth = J * fields * WIN
    packed = depth // 2 + depth // 3
    grid = pl.pallas_call(
        fourier_kernel,
        out_shape=jax.ShapeDtypeStruct((PEERS, packed, LANES), jnp.bfloat16),
        in_specs=[vmem, vmem],
        out_specs=vmem,
        scratch_shapes=[pltpu.VMEM((depth, waves * parts), jnp.float32)],
        compiler_params=pltpu.CompilerParams(vmem_limit_bytes=24 * MIB),
        cost_estimate=pl.CostEstimate(
            flops=2 * depth * waves * parts * PEERS * LANES,
            bytes_accessed=3 * MIB,
            transcendentals=0,
        ),
        name="fourier",
    )(rows_here, table)
    segment = lax.all_to_all(
        grid, ("band", "field"), split_axis=0, concat_axis=0, tiled=True, axis_index_groups=second
    )
    total_fields = XS * ZS * fields
    return pl.pallas_call(
        interp_kernel,
        out_shape=jax.ShapeDtypeStruct((total_fields, rows, cols), jnp.float32),
        in_specs=[vmem] * 5,
        out_specs=vmem,
        scratch_shapes=[
            pltpu.VMEM((PEERS * packed, LANES), jnp.float32),
            pltpu.VMEM((2 * TAPS * TAPS + 1, rows, LANES), jnp.float32),
        ],
        compiler_params=pltpu.CompilerParams(vmem_limit_bytes=24 * MIB),
        cost_estimate=pl.CostEstimate(
            flops=50 * total_fields * rows * LANES, bytes_accessed=2 * MIB, transcendentals=0
        ),
        name="interp",
    )(segment, dep_row, dep_col, frac_row, frac_col)


def solution(mesh):
    return jax.shard_map(
        local,
        mesh=mesh,
        in_specs=(
            P("band", None, "field", None),
            P("band", None, None),
            P(),
            P("band", "field"),
            P("band", "field"),
            P("band", "field"),
            P("band", "field"),
        ),
        out_specs=P(None, "band", "field"),
        check_vma=False,
    )
```

```python
import jax
import jax.numpy as jnp
from jax import lax
from jax.experimental import pallas as pl
from jax.experimental.pallas import tpu as pltpu
from jax.sharding import PartitionSpec as P

NLON = 4608
HW = 2
XS = 4
ZS = 12
J = 3
ZC = ZS // J
PEERS = XS * ZC
TAPS = 2 * HW + 1
WIN = 12
SLAB = 16
QUAD = 4
CHUNKS = 1
WIDE = 64
SPLIT = WIDE - 2 * HW
THIN = 40
LANES = 128
MIB = 1024 * 1024


def legendre_kernel(
    wave_hbm, spec_hbm, leg_hbm, out_ref, wave_ref, spec_buf, leg_buf, pad_ref, small_sem, leg_sem
):
    slots, parts, fields, degrees = spec_buf.shape
    lats = leg_buf.shape[1]
    group = parts * fields
    chunks = leg_sem.shape[0]
    per_chunk = slots // chunks
    wave_copy = pltpu.make_async_copy(wave_hbm, wave_ref, small_sem.at[0])
    spec_copy = pltpu.make_async_copy(spec_hbm, spec_buf, small_sem.at[1])
    spec_copy.start()
    wave_copy.start()
    leg_copies = []
    for c in range(chunks):
        part = pl.ds(c * per_chunk, per_chunk)
        leg_copies.append(
            pltpu.make_async_copy(leg_hbm.at[part], leg_buf.at[part], leg_sem.at[c])
        )
    for copy in leg_copies:
        copy.start()
    first = lax.axis_index("band") * slots
    pad_ref[:8, :] = jnp.zeros((8, LANES), jnp.float32)
    pad_ref[lats:, :] = jnp.zeros((SLAB, LANES), jnp.float32)
    lane_in = lax.broadcasted_iota(jnp.int32, (LANES, LANES), 0)
    lane_out = lax.broadcasted_iota(jnp.int32, (LANES, LANES), 1)
    order = (lane_in % fields) * (LANES // fields) + lane_in // fields
    perm = jnp.where(order == lane_out, 1.0, 0.0).astype(jnp.bfloat16)
    position = lax.broadcasted_iota(jnp.int32, (group, degrees), 1)
    slot_of_lane = lax.broadcasted_iota(jnp.int32, (lats, LANES), 1) // group
    wave_copy.wait()
    spec_copy.wait()
    kept = []
    for s in range(slots):
        part = spec_buf[s].astype(jnp.float32)
        rows = jnp.concatenate([part[0], part[1]], axis=0)
        kept.append(jnp.where(position < degrees - wave_ref[first + s], rows, 0.0))
    weights = jnp.concatenate(kept, axis=0).astype(jnp.bfloat16)
    total = jnp.zeros((lats, LANES), jnp.float32)
    for c in range(chunks):
        leg_copies[c].wait()
        rows = leg_buf[c * per_chunk : (c + 1) * per_chunk].reshape(per_chunk * lats, degrees)
        products = lax.dot_general(
            rows, weights, (((1,), (1,)), ((), ())), preferred_element_type=jnp.float32
        )
        for n in range(per_chunk):
            own = slot_of_lane == c * per_chunk + n
            total = jnp.where(own, products[n * lats : (n + 1) * lats], total)
    four = jnp.dot(total.astype(jnp.bfloat16), perm, preferred_element_type=jnp.float32)
    pad_ref[HW : HW + lats, :] = four
    bands = out_ref.shape[0] // J
    for b in range(bands):
        first_row = b * (lats // bands)
        tile = jnp.concatenate(
            [
                pad_ref[first_row + g * QUAD : first_row + (g + 1) * QUAD, :]
                for g in range(WIN // QUAD)
            ],
            axis=1,
        ).astype(jnp.bfloat16)
        for j in range(J):
            out_ref[b * J + j] = tile


def turn_parts(product):
    quarters = product * (4.0 / NLON)
    nearest = jnp.floor(quarters + 0.5)
    x = (product - nearest * (NLON / 4)) * (2.0 * 3.141592653589793 / NLON)
    square = x * x
    sine = x * (1.0 + square * (-1.0 / 6 + square * (1.0 / 120 + square * (-1.0 / 5040 + square * (1.0 / 362880)))))
    cosine = 1.0 + square * (
        -0.5 + square * (1.0 / 24 + square * (-1.0 / 720 + square * (1.0 / 40320 - square * (1.0 / 3628800))))
    )
    quadrant = nearest.astype(jnp.int32)
    swap = (quadrant & 1) == 1
    cos_value = jnp.where(swap, sine, cosine)
    sin_value = jnp.where(swap, cosine, sine)
    cos_value = jnp.where(((quadrant + 1) & 2) == 2, -cos_value, cos_value)
    sin_value = jnp.where((quadrant & 2) == 2, -sin_value, sin_value)
    return cos_value, sin_value


def fill_table(wave_ref, start_ref, out_ref):
    rows = out_ref.shape[0]
    wave = wave_ref[...]
    lane = lax.broadcasted_iota(jnp.int32, (rows, LANES), 1)
    part = (lax.broadcasted_iota(jnp.int32, (rows, LANES), 0) % 2).astype(jnp.float32)
    weight = jnp.where(wave == 0.0, 1.0, 2.0)
    cos_in, sin_in = turn_parts(wave * lane.astype(jnp.float32))
    cos_out, sin_out = turn_parts(wave * start_ref[...] + part * (NLON // 4))
    cos_out, sin_out = weight * cos_out, weight * sin_out
    for p in range(PEERS):
        out_ref[:, p * LANES : (p + 1) * LANES] = (
            cos_out[:, p : p + 1] * cos_in - sin_out[:, p : p + 1] * sin_in
        ).astype(jnp.bfloat16)


def fourier_kernel(four_ref, table_ref, out_ref, flat_ref):
    bands = four_ref.shape[0] // J
    width = 32
    fields = LANES // width
    per_tile = LANES // width
    for j in range(J):
        for q in range(bands // per_tile):
            blocks = [
                four_ref[(per_tile * q + i) * J + j].astype(jnp.float32) for i in range(per_tile)
            ]
            for f in range(fields):
                row = (j * fields + f) * WIN
                for g in range(WIN // QUAD):
                    lanes = slice(g * LANES + f * width, g * LANES + (f + 1) * width)
                    piece = jnp.concatenate([block[:, lanes] for block in blocks], axis=1)
                    first = row + g * QUAD
                    flat_ref[first : first + QUAD, q * LANES : (q + 1) * LANES] = piece
    flat = flat_ref[...].astype(jnp.bfloat16)
    depth = flat.shape[0]
    half, third = depth // 2, depth // 3
    in_low = lax.broadcasted_iota(jnp.int32, (half, LANES), 1) < WIDE
    lane = lax.broadcasted_iota(jnp.int32, (third, LANES), 1)
    for n in range(PEERS // 2):
        both = jnp.dot(
            flat,
            table_ref[:, 2 * n * LANES : 2 * (n + 1) * LANES],
            preferred_element_type=jnp.float32,
        )
        for m in range(2):
            rows = both[:, m * LANES : (m + 1) * LANES]
            wide = jnp.where(in_low, rows[:half], pltpu.roll(rows[half:], WIDE, 1))
            thins = [
                pltpu.roll(rows[k * third : (k + 1) * third], (k * THIN - SPLIT) % LANES, 1)
                for k in range(3)
            ]
            thin = jnp.where(lane < THIN, thins[0], jnp.where(lane < 2 * THIN, thins[1], thins[2]))
            out_ref[2 * n + m] = jnp.concatenate([wide, thin], axis=0).astype(jnp.bfloat16)


def tables_kernel(
    wave_ref, start_ref, dep_row, dep_col, frac_row, frac_col, table_ref, out_ref, pad_ref
):
    fill_table(wave_ref, start_ref, table_ref)
    rows, cols = dep_row.shape
    row_ids = lax.axis_index("band") * rows + lax.broadcasted_iota(jnp.int32, (rows, cols), 0)
    col_ids = lax.axis_index("field") * cols + lax.broadcasted_iota(jnp.int32, (rows, cols), 1)
    delta_row = dep_row[...] - row_ids
    delta_col = dep_col[...] - col_ids + HW
    delta_col = jnp.where(delta_col < 0, delta_col + NLON, delta_col)
    delta_col = jnp.where(delta_col >= NLON, delta_col - NLON, delta_col) - HW

    def hats(delta, frac):
        return [
            jnp.where(delta == o, 1.0 - frac, 0.0) + jnp.where(delta + 1 == o, frac, 0.0)
            for o in range(-HW, HW + 1)
        ]

    row_hats, col_hats = hats(delta_row, frac_row[...]), hats(delta_col, frac_col[...])
    pad_ref[...] = jnp.zeros_like(pad_ref)
    lane = lax.broadcasted_iota(jnp.int32, (rows, LANES), 1)
    for d in range(TAPS):
        for e in range(TAPS):
            pad_ref[:, :cols] = row_hats[d] * col_hats[e]
            tap = pad_ref[...]
            wide = jnp.where(lane < SPLIT, tap, 0.0)
            thin = pltpu.roll(jnp.where(lane < SPLIT, 0.0, tap), LANES - SPLIT, 1)
            wide = wide + pltpu.roll(wide, WIDE, 1)
            thin = thin + pltpu.roll(thin, THIN, 1) + pltpu.roll(thin, 2 * THIN, 1)
            out_ref[d * TAPS + e] = pltpu.roll(wide, e, 1) if e else wide
            out_ref[TAPS * TAPS + d * TAPS + e] = pltpu.roll(thin, e, 1) if e else thin


def interp_kernel(grid_ref, taps_ref, out_ref, buf):
    rows, cols = out_ref.shape[1:]
    peers, depth = grid_ref.shape[:2]
    per_peer = out_ref.shape[0] // peers
    fields = per_peer // J
    lane = lax.broadcasted_iota(jnp.int32, (rows, LANES), 1)
    for p in range(peers):
        buf[p * depth : (p + 1) * depth, :] = grid_ref[p].astype(jnp.float32)

    def stencils(bases, first_tap):
        sums = [[None] * TAPS for _ in bases]
        for d in range(TAPS):
            planes = [buf[pl.ds(base + d, rows), :] for base in bases]
            for e in range(TAPS):
                tap = taps_ref[first_tap + d * TAPS + e]
                for n, plane in enumerate(planes):
                    term = plane * tap
                    sums[n][e] = term if d == 0 else sums[n][e] + term
        results = []
        for columns in sums:
            result = columns[0]
            for e in range(1, TAPS):
                result = result + pltpu.roll(columns[e], LANES - e, 1)
            results.append(result)
        return results

    def body(p, carry):
        base = pl.multiple_of(p * depth, 8)
        wide = stencils([base + u * WIN for u in range(per_peer // 2)], 0)
        low = base + (per_peer // 2) * WIN
        thin = stencils([low + v * WIN for v in range(per_peer // 3)], TAPS * TAPS)
        for t in range(per_peer):
            left = wide[t % (per_peer // 2)]
            left = pltpu.roll(left, WIDE, 1) if t >= per_peer // 2 else left
            right = thin[t % (per_peer // 3)]
            right = pltpu.roll(right, (SPLIT - THIN * (t // (per_peer // 3))) % LANES, 1)
            z = p // XS + ZC * (t // fields)
            row = ((p % XS) * ZS + z) * fields + t % fields
            out_ref[row] = jnp.where(lane < SPLIT, left, right)[:, :cols]
        return carry

    lax.fori_loop(0, peers, body, 0, unroll=4)


def exchange_groups(bands):
    first, second = [], []
    for x in range(XS):
        for i in range(ZC):
            first.append(
                [b * XS * ZS + x * ZS + i + ZC * j for b in range(bands) for j in range(J)]
            )
    for b in range(bands):
        shift = ZC // 2 if b % 2 and J > 1 else 0
        for g in range(J):
            window = sorted(((ZC * g + shift + n) % ZS for n in range(ZC)), key=lambda z: z % ZC)
            second.append([b * XS * ZS + x * ZS + z for z in window for x in range(XS)])
    return first, second


def local(spectra, legendre, wavenum, dep_row, dep_col, frac_row, frac_col):
    bands = lax.axis_size("band")
    band = lax.axis_index("band")
    field = lax.axis_index("field")
    slots, parts, fields, degrees = spectra.shape
    lats = legendre.shape[1]
    waves = wavenum.shape[0]
    rows, cols = dep_row.shape
    first, second = exchange_groups(bands)
    vmem = pl.BlockSpec(memory_space=pltpu.VMEM)
    hbm = pl.BlockSpec(memory_space=pltpu.HBM)

    four = pl.pallas_call(
        legendre_kernel,
        out_shape=jax.ShapeDtypeStruct((bands * J, QUAD, WIN // QUAD * LANES), jnp.bfloat16),
        in_specs=[hbm, hbm, hbm],
        out_specs=vmem,
        scratch_shapes=[
            pltpu.SMEM(wavenum.shape, jnp.int32),
            pltpu.VMEM(spectra.shape, jnp.bfloat16),
            pltpu.VMEM(legendre.shape, jnp.bfloat16),
            pltpu.VMEM((lats + SLAB, LANES), jnp.float32),
            pltpu.SemaphoreType.DMA((2,)),
            pltpu.SemaphoreType.DMA((CHUNKS,)),
        ],
        compiler_params=pltpu.CompilerParams(vmem_limit_bytes=60 * MIB),
        cost_estimate=pl.CostEstimate(
            flops=2 * slots * LANES * lats * degrees, bytes_accessed=6 * MIB, transcendentals=0
        ),
        name="legendre",
    )(wavenum, spectra, legendre)
    rows_here = lax.all_to_all(
        four, ("band", "field"), split_axis=0, concat_axis=0, tiled=True, axis_index_groups=first
    )

    z_here = field % ZS
    mod_here = z_here % ZC
    shift = jnp.where(band % 2 == 1, ZC // 2 if J > 1 else 0, 0)
    group = (z_here // ZC - jnp.where(mod_here < shift, 1, 0)) % J
    peer = jnp.minimum(lax.iota(jnp.int32, LANES), PEERS - 1)
    mod_peer = peer // XS
    z_peer = (ZC * group + mod_peer + jnp.where(mod_peer < shift, ZC, 0)) % ZS
    start = ((peer % XS) * ZS + z_peer) * cols - HW
    start = jnp.where(start < 0, start + NLON, start)
    wave_rows = jnp.broadcast_to(wavenum[:, None], (waves, parts)).reshape(waves * parts, 1)
    table, taps = pl.pallas_call(
        tables_kernel,
        out_shape=[
            jax.ShapeDtypeStruct((waves * parts, PEERS * LANES), jnp.bfloat16),
            jax.ShapeDtypeStruct((2 * TAPS * TAPS, rows, LANES), jnp.float32),
        ],
        in_specs=[vmem] * 6,
        out_specs=[vmem] * 2,
        scratch_shapes=[pltpu.VMEM((rows, LANES), jnp.float32)],
        compiler_params=pltpu.CompilerParams(vmem_limit_bytes=24 * MIB),
        cost_estimate=pl.CostEstimate(
            flops=20 * MIB, bytes_accessed=4 * MIB, transcendentals=0
        ),
        name="tables",
    )(
        wave_rows.astype(jnp.float32),
        start.astype(jnp.float32)[None, :],
        dep_row,
        dep_col,
        frac_row,
        frac_col,
    )

    depth = J * fields * WIN
    packed = depth // 2 + depth // 3
    grid = pl.pallas_call(
        fourier_kernel,
        out_shape=jax.ShapeDtypeStruct((PEERS, packed, LANES), jnp.bfloat16),
        in_specs=[vmem, vmem],
        out_specs=vmem,
        scratch_shapes=[pltpu.VMEM((depth, waves * parts), jnp.float32)],
        compiler_params=pltpu.CompilerParams(vmem_limit_bytes=24 * MIB),
        cost_estimate=pl.CostEstimate(
            flops=2 * depth * waves * parts * PEERS * LANES,
            bytes_accessed=3 * MIB,
            transcendentals=0,
        ),
        name="fourier",
    )(rows_here, table)
    segment = lax.all_to_all(
        grid, ("band", "field"), split_axis=0, concat_axis=0, tiled=True, axis_index_groups=second
    )
    total_fields = XS * ZS * fields
    return pl.pallas_call(
        interp_kernel,
        out_shape=jax.ShapeDtypeStruct((total_fields, rows, cols), jnp.float32),
        in_specs=[vmem] * 2,
        out_specs=vmem,
        scratch_shapes=[pltpu.VMEM((PEERS * packed, LANES), jnp.float32)],
        compiler_params=pltpu.CompilerParams(vmem_limit_bytes=24 * MIB),
        cost_estimate=pl.CostEstimate(
            flops=50 * total_fields * rows * LANES, bytes_accessed=2 * MIB, transcendentals=0
        ),
        name="interp",
    )(segment, taps)


def solution(mesh):
    return jax.shard_map(
        local,
        mesh=mesh,
        in_specs=(
            P("band", None, "field", None),
            P("band", None, None),
            P(),
            P("band", "field"),
            P("band", "field"),
            P("band", "field"),
            P("band", "field"),
        ),
        out_specs=P(None, "band", "field"),
        check_vma=False,
    )
```

```python
import jax
import jax.numpy as jnp
from jax import lax
from jax.experimental import pallas as pl
from jax.experimental.pallas import tpu as pltpu
from jax.sharding import PartitionSpec as P

NLON = 4608
HW = 2
XS = 4
ZS = 12
J = 3
ZC = ZS // J
PEERS = XS * ZC
TAPS = 2 * HW + 1
WIN = 12
SLAB = 16
QUAD = 4
CHUNK = 768
WIDE = 64
SPLIT = WIDE - 2 * HW
THIN = 40
LANES = 128
MIB = 1024 * 1024


def legendre_kernel(
    wave_hbm,
    spec_hbm,
    leg_hbm,
    out_ref,
    wave_ref,
    spec_buf,
    leg_buf,
    weight_ref,
    sum_ref,
    pad_ref,
    small_sem,
    leg_sem,
):
    slots, parts, fields, degrees = spec_buf.shape
    lats = leg_buf.shape[1]
    group = parts * fields
    wave_copy = pltpu.make_async_copy(wave_hbm, wave_ref, small_sem.at[0])
    spec_copy = pltpu.make_async_copy(spec_hbm, spec_buf, small_sem.at[1])
    wave_copy.start()
    spec_copy.start()
    low_copy = pltpu.make_async_copy(
        leg_hbm.at[:, :, pl.ds(0, CHUNK)], leg_buf.at[:, :, pl.ds(0, CHUNK)], leg_sem.at[0]
    )
    rest = degrees - CHUNK
    high_copy = pltpu.make_async_copy(
        leg_hbm.at[:, :, pl.ds(CHUNK, rest)], leg_buf.at[:, :, pl.ds(CHUNK, rest)], leg_sem.at[1]
    )
    low_copy.start()
    first = lax.axis_index("band") * slots
    pad_ref[:8, :] = jnp.zeros((8, LANES), jnp.float32)
    pad_ref[lats:, :] = jnp.zeros((SLAB, LANES), jnp.float32)
    lane_in = lax.broadcasted_iota(jnp.int32, (LANES, LANES), 0)
    lane_out = lax.broadcasted_iota(jnp.int32, (LANES, LANES), 1)
    order = (lane_in % fields) * (LANES // fields) + lane_in // fields
    perm = jnp.where(order == lane_out, 1.0, 0.0).astype(jnp.bfloat16)
    position = lax.broadcasted_iota(jnp.int32, (group, degrees), 1)
    slot_of_lane = lax.broadcasted_iota(jnp.int32, (lats, LANES), 1) // group
    wave_copy.wait()
    needs_high = degrees - wave_ref[first] > CHUNK

    @pl.when(needs_high)
    def _():
        high_copy.start()

    spec_copy.wait()
    kept = []
    for s in range(slots):
        part = spec_buf[s].astype(jnp.float32)
        rows = jnp.concatenate([part[0], part[1]], axis=0)
        kept.append(jnp.where(position < degrees - wave_ref[first + s], rows, 0.0))
    weight_ref[...] = jnp.concatenate(kept, axis=0).astype(jnp.bfloat16)

    def products_of(start, width):
        return lax.dot_general(
            leg_buf[:, :, start : start + width].reshape(slots * lats, width),
            weight_ref[:, start : start + width],
            (((1,), (1,)), ((), ())),
            preferred_element_type=jnp.float32,
        )

    def own_lanes(products):
        kept_lanes = jnp.zeros((lats, LANES), jnp.float32)
        for s in range(slots):
            part = products[s * lats : (s + 1) * lats]
            kept_lanes = jnp.where(slot_of_lane == s, part, kept_lanes)
        return kept_lanes

    low_copy.wait()
    sum_ref[...] = own_lanes(products_of(0, CHUNK))

    @pl.when(needs_high)
    def _():
        high_copy.wait()
        sum_ref[...] += own_lanes(products_of(CHUNK, rest))

    total = sum_ref[...]
    four = jnp.dot(total.astype(jnp.bfloat16), perm, preferred_element_type=jnp.float32)
    pad_ref[HW : HW + lats, :] = four
    bands = out_ref.shape[0] // J
    for b in range(bands):
        first_row = b * (lats // bands)
        tile = jnp.concatenate(
            [
                pad_ref[first_row + g * QUAD : first_row + (g + 1) * QUAD, :]
                for g in range(WIN // QUAD)
            ],
            axis=1,
        ).astype(jnp.bfloat16)
        for j in range(J):
            out_ref[j * bands + b] = tile


def turn_parts(product):
    quarters = product * (4.0 / NLON)
    nearest = jnp.floor(quarters + 0.5)
    x = (product - nearest * (NLON / 4)) * (2.0 * 3.141592653589793 / NLON)
    square = x * x
    sine = x * (1.0 + square * (-1.0 / 6 + square * (1.0 / 120 + square * (-1.0 / 5040 + square * (1.0 / 362880)))))
    cosine = 1.0 + square * (
        -0.5 + square * (1.0 / 24 + square * (-1.0 / 720 + square * (1.0 / 40320 - square * (1.0 / 3628800))))
    )
    quadrant = nearest.astype(jnp.int32)
    swap = (quadrant & 1) == 1
    cos_value = jnp.where(swap, sine, cosine)
    sin_value = jnp.where(swap, cosine, sine)
    cos_value = jnp.where(((quadrant + 1) & 2) == 2, -cos_value, cos_value)
    sin_value = jnp.where((quadrant & 2) == 2, -sin_value, sin_value)
    return cos_value, sin_value


def fill_table(wave_ref, start_ref, out_ref):
    rows = out_ref.shape[0]
    wave = wave_ref[...]
    lane = lax.broadcasted_iota(jnp.int32, (rows, LANES), 1)
    part = (lax.broadcasted_iota(jnp.int32, (rows, LANES), 0) % 2).astype(jnp.float32)
    weight = jnp.where(wave == 0.0, 1.0, 2.0)
    cos_in, sin_in = turn_parts(wave * lane.astype(jnp.float32))
    cos_out, sin_out = turn_parts(wave * start_ref[...] + part * (NLON // 4))
    cos_out, sin_out = weight * cos_out, weight * sin_out
    for p in range(PEERS):
        out_ref[:, p * LANES : (p + 1) * LANES] = (
            cos_out[:, p : p + 1] * cos_in - sin_out[:, p : p + 1] * sin_in
        ).astype(jnp.bfloat16)


def fourier_kernel(four_ref, table_ref, out_ref, flat_ref):
    bands = four_ref.shape[0] // J
    width = 32
    fields = LANES // width
    per_tile = LANES // width
    for j in range(J):
        for q in range(bands // per_tile):
            blocks = [
                four_ref[j * bands + per_tile * q + i].astype(jnp.float32) for i in range(per_tile)
            ]
            for f in range(fields):
                row = (j * fields + f) * WIN
                for g in range(WIN // QUAD):
                    lanes = slice(g * LANES + f * width, g * LANES + (f + 1) * width)
                    piece = jnp.concatenate([block[:, lanes] for block in blocks], axis=1)
                    first = row + g * QUAD
                    flat_ref[first : first + QUAD, q * LANES : (q + 1) * LANES] = piece
    flat = flat_ref[...].astype(jnp.bfloat16)
    depth = flat.shape[0]
    half, third = depth // 2, depth // 3
    in_low = lax.broadcasted_iota(jnp.int32, (half, LANES), 1) < WIDE
    lane = lax.broadcasted_iota(jnp.int32, (third, LANES), 1)
    for n in range(PEERS // 2):
        both = jnp.dot(
            flat,
            table_ref[:, 2 * n * LANES : 2 * (n + 1) * LANES],
            preferred_element_type=jnp.float32,
        )
        for m in range(2):
            rows = both[:, m * LANES : (m + 1) * LANES]
            wide = jnp.where(in_low, rows[:half], pltpu.roll(rows[half:], WIDE, 1))
            thins = [
                pltpu.roll(rows[k * third : (k + 1) * third], (k * THIN - SPLIT) % LANES, 1)
                for k in range(3)
            ]
            thin = jnp.where(lane < THIN, thins[0], jnp.where(lane < 2 * THIN, thins[1], thins[2]))
            out_ref[2 * n + m] = jnp.concatenate([wide, thin], axis=0).astype(jnp.bfloat16)


def tables_kernel(
    wave_ref, start_ref, dep_row, dep_col, frac_row, frac_col, table_ref, out_ref, pad_ref
):
    fill_table(wave_ref, start_ref, table_ref)
    rows, cols = dep_row.shape
    row_ids = lax.axis_index("band") * rows + lax.broadcasted_iota(jnp.int32, (rows, cols), 0)
    col_ids = lax.axis_index("field") * cols + lax.broadcasted_iota(jnp.int32, (rows, cols), 1)
    delta_row = dep_row[...] - row_ids
    delta_col = dep_col[...] - col_ids + HW
    delta_col = jnp.where(delta_col < 0, delta_col + NLON, delta_col)
    delta_col = jnp.where(delta_col >= NLON, delta_col - NLON, delta_col) - HW

    def hats(delta, frac):
        return [
            jnp.where(delta == o, 1.0 - frac, 0.0) + jnp.where(delta + 1 == o, frac, 0.0)
            for o in range(-HW, HW + 1)
        ]

    row_hats, col_hats = hats(delta_row, frac_row[...]), hats(delta_col, frac_col[...])
    pad_ref[...] = jnp.zeros_like(pad_ref)
    lane = lax.broadcasted_iota(jnp.int32, (rows, LANES), 1)
    for d in range(TAPS):
        for e in range(TAPS):
            pad_ref[:, :cols] = row_hats[d] * col_hats[e]
            tap = pad_ref[...]
            wide = jnp.where(lane < SPLIT, tap, 0.0)
            thin = pltpu.roll(jnp.where(lane < SPLIT, 0.0, tap), LANES - SPLIT, 1)
            wide = wide + pltpu.roll(wide, WIDE, 1)
            thin = thin + pltpu.roll(thin, THIN, 1) + pltpu.roll(thin, 2 * THIN, 1)
            out_ref[d * TAPS + e] = pltpu.roll(wide, e, 1) if e else wide
            out_ref[TAPS * TAPS + d * TAPS + e] = pltpu.roll(thin, e, 1) if e else thin


def interp_kernel(grid_ref, taps_ref, out_hbm, buf, out_ref, out_sem):
    rows, cols = out_ref.shape[1:]
    peers, depth = grid_ref.shape[:2]
    per_peer = out_ref.shape[0] // peers
    fields = per_peer // J
    lane = lax.broadcasted_iota(jnp.int32, (rows, LANES), 1)
    for p in range(peers):
        buf[p * depth : (p + 1) * depth, :] = grid_ref[p].astype(jnp.float32)

    def stencils(bases, first_tap):
        sums = [[None] * TAPS for _ in bases]
        for d in range(TAPS):
            planes = [buf[pl.ds(base + d, rows), :] for base in bases]
            for e in range(TAPS):
                tap = taps_ref[first_tap + d * TAPS + e]
                for n, plane in enumerate(planes):
                    term = plane * tap
                    sums[n][e] = term if d == 0 else sums[n][e] + term
        results = []
        for columns in sums:
            result = columns[0]
            for e in range(1, TAPS):
                result = result + pltpu.roll(columns[e], LANES - e, 1)
            results.append(result)
        return results

    def one_peer(p, x, i):
        base = pl.multiple_of(p * depth, 8)
        wide = stencils([base + u * WIN for u in range(per_peer // 2)], 0)
        low = base + (per_peer // 2) * WIN
        thin = stencils([low + v * WIN for v in range(per_peer // 3)], TAPS * TAPS)
        for t in range(per_peer):
            left = wide[t % (per_peer // 2)]
            left = pltpu.roll(left, WIDE, 1) if t >= per_peer // 2 else left
            right = thin[t % (per_peer // 3)]
            right = pltpu.roll(right, (SPLIT - THIN * (t // (per_peer // 3))) % LANES, 1)
            row = (x * ZS + i + ZC * (t // fields)) * fields + t % fields
            out_ref[row] = jnp.where(lane < SPLIT, left, right)[:, :cols]

    def part_copy(x):
        part = pl.ds(x * (ZS * fields), ZS * fields)
        return pltpu.make_async_copy(out_ref.at[part], out_hbm.at[part], out_sem.at[x])

    def body(x, carry):
        for i in range(ZC):
            one_peer(i * XS + x, x, i)
        part_copy(x).start()
        return carry

    lax.fori_loop(0, XS, body, 0)
    for x in range(XS):
        part_copy(x).wait()


def exchange_groups(bands):
    first, second = [], []
    for x in range(XS):
        for i in range(ZC):
            first.append(
                [b * XS * ZS + x * ZS + i + ZC * j for j in range(J) for b in range(bands)]
            )
    for b in range(bands):
        shift = ZC // 2 if b % 2 and J > 1 else 0
        for g in range(J):
            window = sorted(((ZC * g + shift + n) % ZS for n in range(ZC)), key=lambda z: z % ZC)
            second.append([b * XS * ZS + x * ZS + z for z in window for x in range(XS)])
    return first, second


def local(spectra, legendre, wavenum, dep_row, dep_col, frac_row, frac_col):
    bands = lax.axis_size("band")
    band = lax.axis_index("band")
    field = lax.axis_index("field")
    slots, parts, fields, degrees = spectra.shape
    lats = legendre.shape[1]
    waves = wavenum.shape[0]
    rows, cols = dep_row.shape
    first, second = exchange_groups(bands)
    vmem = pl.BlockSpec(memory_space=pltpu.VMEM)
    hbm = pl.BlockSpec(memory_space=pltpu.HBM)

    four = pl.pallas_call(
        legendre_kernel,
        out_shape=jax.ShapeDtypeStruct((bands * J, QUAD, WIN // QUAD * LANES), jnp.bfloat16),
        in_specs=[hbm, hbm, hbm],
        out_specs=vmem,
        scratch_shapes=[
            pltpu.SMEM(wavenum.shape, jnp.int32),
            pltpu.VMEM(spectra.shape, jnp.bfloat16),
            pltpu.VMEM(legendre.shape, jnp.bfloat16),
            pltpu.VMEM((LANES, degrees), jnp.bfloat16),
            pltpu.VMEM((lats, LANES), jnp.float32),
            pltpu.VMEM((lats + SLAB, LANES), jnp.float32),
            pltpu.SemaphoreType.DMA((2,)),
            pltpu.SemaphoreType.DMA((2,)),
        ],
        compiler_params=pltpu.CompilerParams(vmem_limit_bytes=60 * MIB),
        cost_estimate=pl.CostEstimate(
            flops=2 * slots * LANES * lats * degrees, bytes_accessed=6 * MIB, transcendentals=0
        ),
        name="legendre",
    )(wavenum, spectra, legendre)
    rows_here = lax.all_to_all(
        four, ("band", "field"), split_axis=0, concat_axis=0, tiled=True, axis_index_groups=first
    )

    z_here = field % ZS
    mod_here = z_here % ZC
    shift = jnp.where(band % 2 == 1, ZC // 2 if J > 1 else 0, 0)
    group = (z_here // ZC - jnp.where(mod_here < shift, 1, 0)) % J
    peer = jnp.minimum(lax.iota(jnp.int32, LANES), PEERS - 1)
    mod_peer = peer // XS
    z_peer = (ZC * group + mod_peer + jnp.where(mod_peer < shift, ZC, 0)) % ZS
    start = ((peer % XS) * ZS + z_peer) * cols - HW
    start = jnp.where(start < 0, start + NLON, start)
    wave_rows = jnp.broadcast_to(wavenum[:, None], (waves, parts)).reshape(waves * parts, 1)
    table, taps = pl.pallas_call(
        tables_kernel,
        out_shape=[
            jax.ShapeDtypeStruct((waves * parts, PEERS * LANES), jnp.bfloat16),
            jax.ShapeDtypeStruct((2 * TAPS * TAPS, rows, LANES), jnp.float32),
        ],
        in_specs=[vmem] * 6,
        out_specs=[vmem] * 2,
        scratch_shapes=[pltpu.VMEM((rows, LANES), jnp.float32)],
        compiler_params=pltpu.CompilerParams(vmem_limit_bytes=24 * MIB),
        cost_estimate=pl.CostEstimate(
            flops=20 * MIB, bytes_accessed=4 * MIB, transcendentals=0
        ),
        name="tables",
    )(
        wave_rows.astype(jnp.float32),
        start.astype(jnp.float32)[None, :],
        dep_row,
        dep_col,
        frac_row,
        frac_col,
    )

    depth = J * fields * WIN
    packed = depth // 2 + depth // 3
    grid = pl.pallas_call(
        fourier_kernel,
        out_shape=jax.ShapeDtypeStruct((PEERS, packed, LANES), jnp.bfloat16),
        in_specs=[vmem, vmem],
        out_specs=vmem,
        scratch_shapes=[pltpu.VMEM((depth, waves * parts), jnp.float32)],
        compiler_params=pltpu.CompilerParams(vmem_limit_bytes=24 * MIB),
        cost_estimate=pl.CostEstimate(
            flops=2 * depth * waves * parts * PEERS * LANES,
            bytes_accessed=3 * MIB,
            transcendentals=0,
        ),
        name="fourier",
    )(rows_here, table)
    segment = lax.all_to_all(
        grid, ("band", "field"), split_axis=0, concat_axis=0, tiled=True, axis_index_groups=second
    )
    total_fields = XS * ZS * fields
    return pl.pallas_call(
        interp_kernel,
        out_shape=jax.ShapeDtypeStruct((total_fields, rows, cols), jnp.float32),
        in_specs=[vmem] * 2,
        out_specs=hbm,
        scratch_shapes=[
            pltpu.VMEM((PEERS * packed, LANES), jnp.float32),
            pltpu.VMEM((total_fields, rows, cols), jnp.float32),
            pltpu.SemaphoreType.DMA((XS,)),
        ],
        compiler_params=pltpu.CompilerParams(vmem_limit_bytes=24 * MIB),
        cost_estimate=pl.CostEstimate(
            flops=50 * total_fields * rows * LANES, bytes_accessed=2 * MIB, transcendentals=0
        ),
        name="interp",
    )(segment, taps)


def solution(mesh):
    return jax.shard_map(
        local,
        mesh=mesh,
        in_specs=(
            P("band", None, "field", None),
            P("band", None, None),
            P(),
            P("band", "field"),
            P("band", "field"),
            P("band", "field"),
            P("band", "field"),
        ),
        out_specs=P(None, "band", "field"),
        check_vma=False,
    )
```

```python
import jax
import jax.numpy as jnp
from jax import lax
from jax.experimental import pallas as pl
from jax.experimental.pallas import tpu as pltpu
from jax.sharding import PartitionSpec as P

NLON = 4608
HW = 2
XS = 4
ZS = 12
J = 3
ZC = ZS // J
PEERS = XS * ZC
TAPS = 2 * HW + 1
WIN = 12
SLAB = 16
QUAD = 4
CHUNK = 768
WIDE = 64
SPLIT = WIDE - 2 * HW
THIN = 40
LANES = 128
MIB = 1024 * 1024


def legendre_kernel(
    wave_hbm,
    spec_hbm,
    leg_hbm,
    out_ref,
    wave_ref,
    spec_buf,
    leg_buf,
    weight_ref,
    sum_ref,
    pad_ref,
    small_sem,
    leg_sem,
):
    slots, parts, fields, degrees = spec_buf.shape
    lats = leg_buf.shape[1]
    group = parts * fields
    wave_copy = pltpu.make_async_copy(wave_hbm, wave_ref, small_sem.at[0])
    spec_copy = pltpu.make_async_copy(spec_hbm, spec_buf, small_sem.at[1])
    wave_copy.start()
    spec_copy.start()
    low_copy = pltpu.make_async_copy(
        leg_hbm.at[:, :, pl.ds(0, CHUNK)], leg_buf.at[:, :, pl.ds(0, CHUNK)], leg_sem.at[0]
    )
    rest = degrees - CHUNK
    high_copy = pltpu.make_async_copy(
        leg_hbm.at[:, :, pl.ds(CHUNK, rest)], leg_buf.at[:, :, pl.ds(CHUNK, rest)], leg_sem.at[1]
    )
    low_copy.start()
    first = lax.axis_index("band") * slots
    pad_ref[:8, :] = jnp.zeros((8, LANES), jnp.float32)
    pad_ref[lats:, :] = jnp.zeros((SLAB, LANES), jnp.float32)
    lane_in = lax.broadcasted_iota(jnp.int32, (LANES, LANES), 0)
    lane_out = lax.broadcasted_iota(jnp.int32, (LANES, LANES), 1)
    order = (lane_in % fields) * (LANES // fields) + lane_in // fields
    perm = jnp.where(order == lane_out, 1.0, 0.0).astype(jnp.bfloat16)
    position = lax.broadcasted_iota(jnp.int32, (group, degrees), 1)
    slot_of_lane = lax.broadcasted_iota(jnp.int32, (lats, LANES), 1) // group
    wave_copy.wait()
    needs_high = degrees - wave_ref[first] > CHUNK

    @pl.when(needs_high)
    def _():
        high_copy.start()

    spec_copy.wait()
    kept = []
    for s in range(slots):
        part = spec_buf[s].astype(jnp.float32)
        rows = jnp.concatenate([part[0], part[1]], axis=0)
        kept.append(jnp.where(position < degrees - wave_ref[first + s], rows, 0.0))
    weight_ref[...] = jnp.concatenate(kept, axis=0).astype(jnp.bfloat16)

    def products_of(start, width):
        return lax.dot_general(
            leg_buf[:, :, start : start + width].reshape(slots * lats, width),
            weight_ref[:, start : start + width],
            (((1,), (1,)), ((), ())),
            preferred_element_type=jnp.float32,
        )

    def own_lanes(products):
        kept_lanes = jnp.zeros((lats, LANES), jnp.float32)
        for s in range(slots):
            part = products[s * lats : (s + 1) * lats]
            kept_lanes = jnp.where(slot_of_lane == s, part, kept_lanes)
        return kept_lanes

    low_copy.wait()
    sum_ref[...] = own_lanes(products_of(0, CHUNK))

    @pl.when(needs_high)
    def _():
        high_copy.wait()
        sum_ref[...] += own_lanes(products_of(CHUNK, rest))

    total = sum_ref[...]
    four = jnp.dot(total.astype(jnp.bfloat16), perm, preferred_element_type=jnp.float32)
    pad_ref[HW : HW + lats, :] = four
    bands = out_ref.shape[0] // J
    for b in range(bands):
        first_row = b * (lats // bands)
        tile = jnp.concatenate(
            [
                pad_ref[first_row + g * QUAD : first_row + (g + 1) * QUAD, :]
                for g in range(WIN // QUAD)
            ],
            axis=1,
        ).astype(jnp.bfloat16)
        for j in range(J):
            out_ref[j * bands + b] = tile


def turn_parts(product):
    quarters = product * (4.0 / NLON)
    nearest = jnp.floor(quarters + 0.5)
    x = (product - nearest * (NLON / 4)) * (2.0 * 3.141592653589793 / NLON)
    square = x * x
    sine = x * (1.0 + square * (-1.0 / 6 + square * (1.0 / 120 + square * (-1.0 / 5040 + square * (1.0 / 362880)))))
    cosine = 1.0 + square * (
        -0.5 + square * (1.0 / 24 + square * (-1.0 / 720 + square * (1.0 / 40320 - square * (1.0 / 3628800))))
    )
    quadrant = nearest.astype(jnp.int32)
    swap = (quadrant & 1) == 1
    cos_value = jnp.where(swap, sine, cosine)
    sin_value = jnp.where(swap, cosine, sine)
    cos_value = jnp.where(((quadrant + 1) & 2) == 2, -cos_value, cos_value)
    sin_value = jnp.where((quadrant & 2) == 2, -sin_value, sin_value)
    return cos_value, sin_value


def fill_table(wave_ref, start_ref, out_ref):
    rows = out_ref.shape[0]
    wave = wave_ref[...]
    lane = lax.broadcasted_iota(jnp.int32, (rows, LANES), 1)
    part = (lax.broadcasted_iota(jnp.int32, (rows, LANES), 0) % 2).astype(jnp.float32)
    weight = jnp.where(wave == 0.0, 1.0, 2.0)
    cos_in, sin_in = turn_parts(wave * lane.astype(jnp.float32))
    cos_out, sin_out = turn_parts(wave * start_ref[...] + part * (NLON // 4))
    cos_out, sin_out = weight * cos_out, weight * sin_out
    for p in range(PEERS):
        out_ref[:, p * LANES : (p + 1) * LANES] = (
            cos_out[:, p : p + 1] * cos_in - sin_out[:, p : p + 1] * sin_in
        ).astype(jnp.bfloat16)


def fourier_kernel(four_ref, table_ref, out_ref, flat_ref):
    bands = four_ref.shape[0] // J
    width = 32
    fields = LANES // width
    per_tile = LANES // width
    for j in range(J):
        for q in range(bands // per_tile):
            blocks = [
                four_ref[j * bands + per_tile * q + i].astype(jnp.float32) for i in range(per_tile)
            ]
            for f in range(fields):
                row = (j * fields + f) * WIN
                for g in range(WIN // QUAD):
                    lanes = slice(g * LANES + f * width, g * LANES + (f + 1) * width)
                    piece = jnp.concatenate([block[:, lanes] for block in blocks], axis=1)
                    first = row + g * QUAD
                    flat_ref[first : first + QUAD, q * LANES : (q + 1) * LANES] = piece
    flat = flat_ref[...].astype(jnp.bfloat16)
    depth = flat.shape[0]
    half, third = depth // 2, depth // 3
    in_low = lax.broadcasted_iota(jnp.int32, (half, LANES), 1) < WIDE
    lane = lax.broadcasted_iota(jnp.int32, (third, LANES), 1)
    for n in range(PEERS // 2):
        both = jnp.dot(
            flat,
            table_ref[:, 2 * n * LANES : 2 * (n + 1) * LANES],
            preferred_element_type=jnp.float32,
        )
        for m in range(2):
            rows = both[:, m * LANES : (m + 1) * LANES]
            wide = jnp.where(in_low, rows[:half], pltpu.roll(rows[half:], WIDE, 1))
            thins = [
                pltpu.roll(rows[k * third : (k + 1) * third], (k * THIN - SPLIT) % LANES, 1)
                for k in range(3)
            ]
            thin = jnp.where(lane < THIN, thins[0], jnp.where(lane < 2 * THIN, thins[1], thins[2]))
            out_ref[2 * n + m] = jnp.concatenate([wide, thin], axis=0).astype(jnp.bfloat16)


def tables_kernel(
    wave_ref, start_ref, dep_row, dep_col, frac_row, frac_col, table_ref, out_ref, pad_ref
):
    fill_table(wave_ref, start_ref, table_ref)
    rows, cols = dep_row.shape
    row_ids = lax.axis_index("band") * rows + lax.broadcasted_iota(jnp.int32, (rows, cols), 0)
    col_ids = lax.axis_index("field") * cols + lax.broadcasted_iota(jnp.int32, (rows, cols), 1)
    delta_row = dep_row[...] - row_ids
    delta_col = dep_col[...] - col_ids + HW
    delta_col = jnp.where(delta_col < 0, delta_col + NLON, delta_col)
    delta_col = jnp.where(delta_col >= NLON, delta_col - NLON, delta_col) - HW

    def hats(delta, frac):
        return [
            jnp.where(delta == o, 1.0 - frac, 0.0) + jnp.where(delta + 1 == o, frac, 0.0)
            for o in range(-HW, HW + 1)
        ]

    row_hats, col_hats = hats(delta_row, frac_row[...]), hats(delta_col, frac_col[...])
    pad_ref[...] = jnp.zeros_like(pad_ref)
    lane = lax.broadcasted_iota(jnp.int32, (rows, LANES), 1)
    for d in range(TAPS):
        for e in range(TAPS):
            pad_ref[:, :cols] = row_hats[d] * col_hats[e]
            tap = pad_ref[...]
            wide = jnp.where(lane < SPLIT, tap, 0.0)
            thin = pltpu.roll(jnp.where(lane < SPLIT, 0.0, tap), LANES - SPLIT, 1)
            wide = wide + pltpu.roll(wide, WIDE, 1)
            thin = thin + pltpu.roll(thin, THIN, 1) + pltpu.roll(thin, 2 * THIN, 1)
            out_ref[d * TAPS + e] = pltpu.roll(wide, e, 1) if e else wide
            out_ref[TAPS * TAPS + d * TAPS + e] = pltpu.roll(thin, e, 1) if e else thin


def interp_kernel(grid_ref, taps_ref, out_hbm, buf, out_ref, out_sem):
    rows, cols = out_ref.shape[1:]
    peers, depth = grid_ref.shape[:2]
    per_peer = out_ref.shape[0] // peers
    fields = per_peer // J
    lane = lax.broadcasted_iota(jnp.int32, (rows, LANES), 1)
    for p in range(peers):
        buf[p * depth : (p + 1) * depth, :] = grid_ref[p].astype(jnp.float32)

    def stencils(bases, first_tap):
        sums = [[None] * TAPS for _ in bases]
        for d in range(TAPS):
            planes = [buf[pl.ds(base + d, rows), :] for base in bases]
            for e in range(TAPS):
                tap = taps_ref[first_tap + d * TAPS + e]
                for n, plane in enumerate(planes):
                    term = plane * tap
                    sums[n][e] = term if d == 0 else sums[n][e] + term
        results = []
        for columns in sums:
            result = columns[TAPS - 1]
            for e in range(TAPS - 2, -1, -1):
                result = columns[e] + pltpu.roll(result, LANES - 1, 1)
            results.append(result)
        return results

    def one_peer(p, x, i):
        base = pl.multiple_of(p * depth, 8)
        wide = stencils([base + u * WIN for u in range(per_peer // 2)], 0)
        low = base + (per_peer // 2) * WIN
        thin = stencils([low + v * WIN for v in range(per_peer // 3)], TAPS * TAPS)
        for t in range(per_peer):
            left = wide[t % (per_peer // 2)]
            left = pltpu.roll(left, WIDE, 1) if t >= per_peer // 2 else left
            right = thin[t % (per_peer // 3)]
            right = pltpu.roll(right, (SPLIT - THIN * (t // (per_peer // 3))) % LANES, 1)
            row = (x * ZS + i + ZC * (t // fields)) * fields + t % fields
            out_ref[row] = jnp.where(lane < SPLIT, left, right)[:, :cols]

    def part_copy(x):
        part = pl.ds(x * (ZS * fields), ZS * fields)
        return pltpu.make_async_copy(out_ref.at[part], out_hbm.at[part], out_sem.at[x])

    def body(x, carry):
        for i in range(ZC):
            one_peer(i * XS + x, x, i)
        part_copy(x).start()
        return carry

    lax.fori_loop(0, XS, body, 0, unroll=True)
    for x in range(XS):
        part_copy(x).wait()


def exchange_groups(bands):
    first, second = [], []
    for x in range(XS):
        for i in range(ZC):
            first.append(
                [b * XS * ZS + x * ZS + i + ZC * j for j in range(J) for b in range(bands)]
            )
    for b in range(bands):
        shift = ZC // 2 if b % 2 and J > 1 else 0
        for g in range(J):
            window = sorted(((ZC * g + shift + n) % ZS for n in range(ZC)), key=lambda z: z % ZC)
            second.append([b * XS * ZS + x * ZS + z for z in window for x in range(XS)])
    return first, second


def local(spectra, legendre, wavenum, dep_row, dep_col, frac_row, frac_col):
    bands = lax.axis_size("band")
    band = lax.axis_index("band")
    field = lax.axis_index("field")
    slots, parts, fields, degrees = spectra.shape
    lats = legendre.shape[1]
    waves = wavenum.shape[0]
    rows, cols = dep_row.shape
    first, second = exchange_groups(bands)
    vmem = pl.BlockSpec(memory_space=pltpu.VMEM)
    hbm = pl.BlockSpec(memory_space=pltpu.HBM)

    four = pl.pallas_call(
        legendre_kernel,
        out_shape=jax.ShapeDtypeStruct((bands * J, QUAD, WIN // QUAD * LANES), jnp.bfloat16),
        in_specs=[hbm, hbm, hbm],
        out_specs=vmem,
        scratch_shapes=[
            pltpu.SMEM(wavenum.shape, jnp.int32),
            pltpu.VMEM(spectra.shape, jnp.bfloat16),
            pltpu.VMEM(legendre.shape, jnp.bfloat16),
            pltpu.VMEM((LANES, degrees), jnp.bfloat16),
            pltpu.VMEM((lats, LANES), jnp.float32),
            pltpu.VMEM((lats + SLAB, LANES), jnp.float32),
            pltpu.SemaphoreType.DMA((2,)),
            pltpu.SemaphoreType.DMA((2,)),
        ],
        compiler_params=pltpu.CompilerParams(vmem_limit_bytes=60 * MIB),
        cost_estimate=pl.CostEstimate(
            flops=2 * slots * LANES * lats * degrees, bytes_accessed=6 * MIB, transcendentals=0
        ),
        name="legendre",
    )(wavenum, spectra, legendre)
    rows_here = lax.all_to_all(
        four, ("band", "field"), split_axis=0, concat_axis=0, tiled=True, axis_index_groups=first
    )

    z_here = field % ZS
    mod_here = z_here % ZC
    shift = jnp.where(band % 2 == 1, ZC // 2 if J > 1 else 0, 0)
    group = (z_here // ZC - jnp.where(mod_here < shift, 1, 0)) % J
    peer = jnp.minimum(lax.iota(jnp.int32, LANES), PEERS - 1)
    mod_peer = peer // XS
    z_peer = (ZC * group + mod_peer + jnp.where(mod_peer < shift, ZC, 0)) % ZS
    start = ((peer % XS) * ZS + z_peer) * cols - HW
    start = jnp.where(start < 0, start + NLON, start)
    wave_rows = jnp.broadcast_to(wavenum[:, None], (waves, parts)).reshape(waves * parts, 1)
    table, taps = pl.pallas_call(
        tables_kernel,
        out_shape=[
            jax.ShapeDtypeStruct((waves * parts, PEERS * LANES), jnp.bfloat16),
            jax.ShapeDtypeStruct((2 * TAPS * TAPS, rows, LANES), jnp.float32),
        ],
        in_specs=[vmem] * 6,
        out_specs=[vmem] * 2,
        scratch_shapes=[pltpu.VMEM((rows, LANES), jnp.float32)],
        compiler_params=pltpu.CompilerParams(vmem_limit_bytes=24 * MIB),
        cost_estimate=pl.CostEstimate(
            flops=20 * MIB, bytes_accessed=4 * MIB, transcendentals=0
        ),
        name="tables",
    )(
        wave_rows.astype(jnp.float32),
        start.astype(jnp.float32)[None, :],
        dep_row,
        dep_col,
        frac_row,
        frac_col,
    )

    depth = J * fields * WIN
    packed = depth // 2 + depth // 3
    grid = pl.pallas_call(
        fourier_kernel,
        out_shape=jax.ShapeDtypeStruct((PEERS, packed, LANES), jnp.bfloat16),
        in_specs=[vmem, vmem],
        out_specs=vmem,
        scratch_shapes=[pltpu.VMEM((depth, waves * parts), jnp.float32)],
        compiler_params=pltpu.CompilerParams(vmem_limit_bytes=24 * MIB),
        cost_estimate=pl.CostEstimate(
            flops=2 * depth * waves * parts * PEERS * LANES,
            bytes_accessed=3 * MIB,
            transcendentals=0,
        ),
        name="fourier",
    )(rows_here, table)
    segment = lax.all_to_all(
        grid, ("band", "field"), split_axis=0, concat_axis=0, tiled=True, axis_index_groups=second
    )
    total_fields = XS * ZS * fields
    return pl.pallas_call(
        interp_kernel,
        out_shape=jax.ShapeDtypeStruct((total_fields, rows, cols), jnp.float32),
        in_specs=[vmem] * 2,
        out_specs=hbm,
        scratch_shapes=[
            pltpu.VMEM((PEERS * packed, LANES), jnp.float32),
            pltpu.VMEM((total_fields, rows, cols), jnp.float32),
            pltpu.SemaphoreType.DMA((XS,)),
        ],
        compiler_params=pltpu.CompilerParams(vmem_limit_bytes=24 * MIB),
        cost_estimate=pl.CostEstimate(
            flops=50 * total_fields * rows * LANES, bytes_accessed=2 * MIB, transcendentals=0
        ),
        name="interp",
    )(segment, taps)


def solution(mesh):
    return jax.shard_map(
        local,
        mesh=mesh,
        in_specs=(
            P("band", None, "field", None),
            P("band", None, None),
            P(),
            P("band", "field"),
            P("band", "field"),
            P("band", "field"),
            P("band", "field"),
        ),
        out_specs=P(None, "band", "field"),
        check_vma=False,
    )
```

```python
import jax
import jax.numpy as jnp
from jax import lax
from jax.experimental import pallas as pl
from jax.experimental.pallas import tpu as pltpu
from jax.sharding import PartitionSpec as P

NLON = 4608
HW = 2
XS = 4
ZS = 12
J = 3
ZC = ZS // J
PEERS = XS * ZC
TAPS = 2 * HW + 1
WIN = 12
SLAB = 16
QUAD = 4
CHUNK = 768
WIDE = 64
SPLIT = WIDE - 2 * HW
THIN = 40
LANES = 128
MIB = 1024 * 1024


def legendre_kernel(
    wave_hbm,
    spec_hbm,
    leg_hbm,
    out_ref,
    wave_ref,
    spec_buf,
    leg_buf,
    weight_ref,
    sum_ref,
    pad_ref,
    small_sem,
    leg_sem,
):
    slots, parts, fields, degrees = spec_buf.shape
    lats = leg_buf.shape[1]
    group = parts * fields
    wave_copy = pltpu.make_async_copy(wave_hbm, wave_ref, small_sem.at[0])
    spec_copy = pltpu.make_async_copy(spec_hbm, spec_buf, small_sem.at[1])
    wave_copy.start()
    spec_copy.start()
    low_copy = pltpu.make_async_copy(
        leg_hbm.at[:, :, pl.ds(0, CHUNK)], leg_buf.at[:, :, pl.ds(0, CHUNK)], leg_sem.at[0]
    )
    rest = degrees - CHUNK
    high_copy = pltpu.make_async_copy(
        leg_hbm.at[:, :, pl.ds(CHUNK, rest)], leg_buf.at[:, :, pl.ds(CHUNK, rest)], leg_sem.at[1]
    )
    low_copy.start()
    first = lax.axis_index("band") * slots
    pad_ref[:8, :] = jnp.zeros((8, LANES), jnp.float32)
    pad_ref[lats:, :] = jnp.zeros((SLAB, LANES), jnp.float32)
    lane_in = lax.broadcasted_iota(jnp.int32, (LANES, LANES), 0)
    lane_out = lax.broadcasted_iota(jnp.int32, (LANES, LANES), 1)
    order = (lane_in % fields) * (LANES // fields) + lane_in // fields
    perm = jnp.where(order == lane_out, 1.0, 0.0).astype(jnp.bfloat16)
    position = lax.broadcasted_iota(jnp.int32, (group, degrees), 1)
    slot_of_lane = lax.broadcasted_iota(jnp.int32, (lats, LANES), 1) // group
    wave_copy.wait()
    needs_high = degrees - wave_ref[first] > CHUNK

    @pl.when(needs_high)
    def _():
        high_copy.start()

    spec_copy.wait()
    kept = []
    for s in range(slots):
        part = spec_buf[s].astype(jnp.float32)
        rows = jnp.concatenate([part[0], part[1]], axis=0)
        kept.append(jnp.where(position < degrees - wave_ref[first + s], rows, 0.0))
    weight_ref[...] = jnp.concatenate(kept, axis=0).astype(jnp.bfloat16)

    def products_of(start, width):
        return lax.dot_general(
            leg_buf[:, :, start : start + width].reshape(slots * lats, width),
            weight_ref[:, start : start + width],
            (((1,), (1,)), ((), ())),
            preferred_element_type=jnp.float32,
        )

    def own_lanes(products):
        kept_lanes = jnp.zeros((lats, LANES), jnp.float32)
        for s in range(slots):
            part = products[s * lats : (s + 1) * lats]
            kept_lanes = jnp.where(slot_of_lane == s, part, kept_lanes)
        return kept_lanes

    low_copy.wait()
    sum_ref[...] = own_lanes(products_of(0, CHUNK))

    @pl.when(needs_high)
    def _():
        high_copy.wait()
        sum_ref[...] += own_lanes(products_of(CHUNK, rest))

    total = sum_ref[...]
    four = jnp.dot(total.astype(jnp.bfloat16), perm, preferred_element_type=jnp.float32)
    pad_ref[HW : HW + lats, :] = four
    bands = out_ref.shape[0] // J
    for b in range(bands):
        first_row = b * (lats // bands)
        tile = jnp.concatenate(
            [
                pad_ref[first_row + g * QUAD : first_row + (g + 1) * QUAD, :]
                for g in range(WIN // QUAD)
            ],
            axis=1,
        ).astype(jnp.bfloat16)
        for j in range(J):
            out_ref[j * bands + b] = tile


def turn_parts(product):
    quarters = product * (4.0 / NLON)
    nearest = jnp.floor(quarters + 0.5)
    x = (product - nearest * (NLON / 4)) * (2.0 * 3.141592653589793 / NLON)
    square = x * x
    sine = x * (1.0 + square * (-1.0 / 6 + square * (1.0 / 120 + square * (-1.0 / 5040 + square * (1.0 / 362880)))))
    cosine = 1.0 + square * (
        -0.5 + square * (1.0 / 24 + square * (-1.0 / 720 + square * (1.0 / 40320 - square * (1.0 / 3628800))))
    )
    quadrant = nearest.astype(jnp.int32)
    swap = (quadrant & 1) == 1
    cos_value = jnp.where(swap, sine, cosine)
    sin_value = jnp.where(swap, cosine, sine)
    cos_value = jnp.where(((quadrant + 1) & 2) == 2, -cos_value, cos_value)
    sin_value = jnp.where((quadrant & 2) == 2, -sin_value, sin_value)
    return cos_value, sin_value


def fill_table(wave_ref, start_ref, out_ref):
    rows = out_ref.shape[0]
    wave = wave_ref[...]
    lane = lax.broadcasted_iota(jnp.int32, (rows, LANES), 1)
    part = (lax.broadcasted_iota(jnp.int32, (rows, LANES), 0) % 2).astype(jnp.float32)
    weight = jnp.where(wave == 0.0, 1.0, 2.0)
    cos_in, sin_in = turn_parts(wave * lane.astype(jnp.float32))
    cos_out, sin_out = turn_parts(wave * start_ref[...] + part * (NLON // 4))
    cos_out, sin_out = weight * cos_out, weight * sin_out
    for p in range(PEERS):
        out_ref[:, p * LANES : (p + 1) * LANES] = (
            cos_out[:, p : p + 1] * cos_in - sin_out[:, p : p + 1] * sin_in
        ).astype(jnp.bfloat16)


def fourier_kernel(four_ref, table_ref, out_ref, flat_ref):
    bands = four_ref.shape[0] // J
    width = 32
    fields = LANES // width
    per_tile = LANES // width
    for j in range(J):
        for q in range(bands // per_tile):
            blocks = [
                four_ref[j * bands + per_tile * q + i].astype(jnp.float32) for i in range(per_tile)
            ]
            for f in range(fields):
                row = (j * fields + f) * WIN
                for g in range(WIN // QUAD):
                    lanes = slice(g * LANES + f * width, g * LANES + (f + 1) * width)
                    piece = jnp.concatenate([block[:, lanes] for block in blocks], axis=1)
                    first = row + g * QUAD
                    flat_ref[first : first + QUAD, q * LANES : (q + 1) * LANES] = piece
    flat = flat_ref[...].astype(jnp.bfloat16)
    depth = flat.shape[0]
    half, third = depth // 2, depth // 3
    in_low = lax.broadcasted_iota(jnp.int32, (half, LANES), 1) < WIDE
    lane = lax.broadcasted_iota(jnp.int32, (third, LANES), 1)
    for n in range(PEERS // 2):
        both = jnp.dot(
            flat,
            table_ref[:, 2 * n * LANES : 2 * (n + 1) * LANES],
            preferred_element_type=jnp.float32,
        )
        for m in range(2):
            rows = both[:, m * LANES : (m + 1) * LANES]
            wide = jnp.where(in_low, rows[:half], pltpu.roll(rows[half:], WIDE, 1))
            thins = [
                pltpu.roll(rows[k * third : (k + 1) * third], (k * THIN - SPLIT) % LANES, 1)
                for k in range(3)
            ]
            thin = jnp.where(lane < THIN, thins[0], jnp.where(lane < 2 * THIN, thins[1], thins[2]))
            out_ref[2 * n + m] = jnp.concatenate([wide, thin], axis=0).astype(jnp.bfloat16)


def tables_kernel(
    wave_ref, start_ref, dep_row, dep_col, frac_row, frac_col, table_ref, out_ref, pad_ref
):
    fill_table(wave_ref, start_ref, table_ref)
    rows, cols = dep_row.shape
    row_ids = lax.axis_index("band") * rows + lax.broadcasted_iota(jnp.int32, (rows, cols), 0)
    col_ids = lax.axis_index("field") * cols + lax.broadcasted_iota(jnp.int32, (rows, cols), 1)
    delta_row = dep_row[...] - row_ids
    delta_col = dep_col[...] - col_ids + HW
    delta_col = jnp.where(delta_col < 0, delta_col + NLON, delta_col)
    delta_col = jnp.where(delta_col >= NLON, delta_col - NLON, delta_col) - HW

    def hats(delta, frac):
        return [
            jnp.where(delta == o, 1.0 - frac, 0.0) + jnp.where(delta + 1 == o, frac, 0.0)
            for o in range(-HW, HW + 1)
        ]

    row_hats, col_hats = hats(delta_row, frac_row[...]), hats(delta_col, frac_col[...])
    pad_ref[...] = jnp.zeros_like(pad_ref)
    lane = lax.broadcasted_iota(jnp.int32, (rows, LANES), 1)
    for d in range(TAPS):
        for e in range(TAPS):
            pad_ref[:, :cols] = row_hats[d] * col_hats[e]
            tap = pad_ref[...]
            wide = jnp.where(lane < SPLIT, tap, 0.0)
            thin = pltpu.roll(jnp.where(lane < SPLIT, 0.0, tap), LANES - SPLIT, 1)
            wide = wide + pltpu.roll(wide, WIDE, 1)
            thin = thin + pltpu.roll(thin, THIN, 1) + pltpu.roll(thin, 2 * THIN, 1)
            out_ref[d * TAPS + e] = pltpu.roll(wide, e, 1) if e else wide
            out_ref[TAPS * TAPS + d * TAPS + e] = pltpu.roll(thin, e, 1) if e else thin


def interp_kernel(grid_ref, taps_ref, out_hbm, buf, out_ref, out_sem):
    rows, cols = out_ref.shape[1:]
    peers, depth = grid_ref.shape[:2]
    per_peer = out_ref.shape[0] // peers
    fields = per_peer // J
    lane = lax.broadcasted_iota(jnp.int32, (rows, LANES), 1)
    for p in range(peers):
        buf[p * depth : (p + 1) * depth, :] = grid_ref[p].astype(jnp.float32)

    def stencils(bases, first_tap):
        sums = [[None] * TAPS for _ in bases]
        for d in range(TAPS):
            planes = [buf[pl.ds(base + d, rows), :] for base in bases]
            for e in range(TAPS):
                tap = taps_ref[first_tap + d * TAPS + e]
                for n, plane in enumerate(planes):
                    term = plane * tap
                    sums[n][e] = term if d == 0 else sums[n][e] + term
        results = []
        for columns in sums:
            result = columns[TAPS - 1]
            for e in range(TAPS - 2, -1, -1):
                result = columns[e] + pltpu.roll(result, LANES - 1, 1)
            results.append(result)
        return results

    def one_peer(p, x, i):
        base = pl.multiple_of(p * depth, 8)
        wide = stencils([base + u * WIN for u in range(per_peer // 2)], 0)
        low = base + (per_peer // 2) * WIN
        thin = stencils([low + v * WIN for v in range(per_peer // 3)], TAPS * TAPS)
        for t in range(per_peer):
            left = wide[t % (per_peer // 2)]
            left = pltpu.roll(left, WIDE, 1) if t >= per_peer // 2 else left
            right = thin[t % (per_peer // 3)]
            right = pltpu.roll(right, (SPLIT - THIN * (t // (per_peer // 3))) % LANES, 1)
            row = (x * ZS + i + ZC * (t // fields)) * fields + t % fields
            out_ref[row] = jnp.where(lane < SPLIT, left, right)[:, :cols]

    def part_copy(x):
        part = pl.ds(x * (ZS * fields), ZS * fields)
        return pltpu.make_async_copy(out_ref.at[part], out_hbm.at[part], out_sem.at[x])

    def body(x, carry):
        for i in range(ZC):
            one_peer(i * XS + x, x, i)
        part_copy(x).start()
        return carry

    lax.fori_loop(0, XS, body, 0)
    for x in range(XS):
        part_copy(x).wait()


def exchange_groups(bands):
    first, second = [], []
    for x in range(XS):
        for i in range(ZC):
            first.append(
                [b * XS * ZS + x * ZS + i + ZC * j for j in range(J) for b in range(bands)]
            )
    for b in range(bands):
        shift = ZC // 2 if b % 2 and J > 1 else 0
        for g in range(J):
            window = sorted(((ZC * g + shift + n) % ZS for n in range(ZC)), key=lambda z: z % ZC)
            second.append([b * XS * ZS + x * ZS + z for z in window for x in range(XS)])
    return first, second


def local(spectra, legendre, wavenum, dep_row, dep_col, frac_row, frac_col):
    bands = lax.axis_size("band")
    band = lax.axis_index("band")
    field = lax.axis_index("field")
    slots, parts, fields, degrees = spectra.shape
    lats = legendre.shape[1]
    waves = wavenum.shape[0]
    rows, cols = dep_row.shape
    first, second = exchange_groups(bands)
    vmem = pl.BlockSpec(memory_space=pltpu.VMEM)
    hbm = pl.BlockSpec(memory_space=pltpu.HBM)

    four = pl.pallas_call(
        legendre_kernel,
        out_shape=jax.ShapeDtypeStruct((bands * J, QUAD, WIN // QUAD * LANES), jnp.bfloat16),
        in_specs=[hbm, hbm, hbm],
        out_specs=vmem,
        scratch_shapes=[
            pltpu.SMEM(wavenum.shape, jnp.int32),
            pltpu.VMEM(spectra.shape, jnp.bfloat16),
            pltpu.VMEM(legendre.shape, jnp.bfloat16),
            pltpu.VMEM((LANES, degrees), jnp.bfloat16),
            pltpu.VMEM((lats, LANES), jnp.float32),
            pltpu.VMEM((lats + SLAB, LANES), jnp.float32),
            pltpu.SemaphoreType.DMA((2,)),
            pltpu.SemaphoreType.DMA((2,)),
        ],
        compiler_params=pltpu.CompilerParams(vmem_limit_bytes=60 * MIB),
        cost_estimate=pl.CostEstimate(
            flops=2 * slots * LANES * lats * degrees, bytes_accessed=6 * MIB, transcendentals=0
        ),
        name="legendre",
    )(wavenum, spectra, legendre)
    rows_here = lax.all_to_all(
        four, ("band", "field"), split_axis=0, concat_axis=0, tiled=True, axis_index_groups=first
    )

    z_here = field % ZS
    mod_here = z_here % ZC
    shift = jnp.where(band % 2 == 1, ZC // 2 if J > 1 else 0, 0)
    group = (z_here // ZC - jnp.where(mod_here < shift, 1, 0)) % J
    peer = jnp.minimum(lax.iota(jnp.int32, LANES), PEERS - 1)
    mod_peer = peer // XS
    z_peer = (ZC * group + mod_peer + jnp.where(mod_peer < shift, ZC, 0)) % ZS
    start = ((peer % XS) * ZS + z_peer) * cols - HW
    start = jnp.where(start < 0, start + NLON, start)
    wave_rows = jnp.broadcast_to(wavenum[:, None], (waves, parts)).reshape(waves * parts, 1)
    table, taps = pl.pallas_call(
        tables_kernel,
        out_shape=[
            jax.ShapeDtypeStruct((waves * parts, PEERS * LANES), jnp.bfloat16),
            jax.ShapeDtypeStruct((2 * TAPS * TAPS, rows, LANES), jnp.float32),
        ],
        in_specs=[vmem] * 6,
        out_specs=[vmem] * 2,
        scratch_shapes=[pltpu.VMEM((rows, LANES), jnp.float32)],
        compiler_params=pltpu.CompilerParams(vmem_limit_bytes=24 * MIB),
        cost_estimate=pl.CostEstimate(
            flops=20 * MIB, bytes_accessed=4 * MIB, transcendentals=0
        ),
        name="tables",
    )(
        wave_rows.astype(jnp.float32),
        start.astype(jnp.float32)[None, :],
        dep_row,
        dep_col,
        frac_row,
        frac_col,
    )

    depth = J * fields * WIN
    packed = depth // 2 + depth // 3
    grid = pl.pallas_call(
        fourier_kernel,
        out_shape=jax.ShapeDtypeStruct((PEERS, packed, LANES), jnp.bfloat16),
        in_specs=[vmem, vmem],
        out_specs=vmem,
        scratch_shapes=[pltpu.VMEM((depth, waves * parts), jnp.float32)],
        compiler_params=pltpu.CompilerParams(vmem_limit_bytes=24 * MIB),
        cost_estimate=pl.CostEstimate(
            flops=2 * depth * waves * parts * PEERS * LANES,
            bytes_accessed=3 * MIB,
            transcendentals=0,
        ),
        name="fourier",
    )(rows_here, table)
    segment = lax.all_to_all(
        grid, ("band", "field"), split_axis=0, concat_axis=0, tiled=True, axis_index_groups=second
    )
    total_fields = XS * ZS * fields
    return pl.pallas_call(
        interp_kernel,
        out_shape=jax.ShapeDtypeStruct((total_fields, rows, cols), jnp.float32),
        in_specs=[vmem] * 2,
        out_specs=hbm,
        scratch_shapes=[
            pltpu.VMEM((PEERS * packed, LANES), jnp.float32),
            pltpu.VMEM((total_fields, rows, cols), jnp.float32),
            pltpu.SemaphoreType.DMA((XS,)),
        ],
        compiler_params=pltpu.CompilerParams(vmem_limit_bytes=24 * MIB),
        cost_estimate=pl.CostEstimate(
            flops=50 * total_fields * rows * LANES, bytes_accessed=2 * MIB, transcendentals=0
        ),
        name="interp",
    )(segment, taps)


def solution(mesh):
    return jax.shard_map(
        local,
        mesh=mesh,
        in_specs=(
            P("band", None, "field", None),
            P("band", None, None),
            P(),
            P("band", "field"),
            P("band", "field"),
            P("band", "field"),
            P("band", "field"),
        ),
        out_specs=P(None, "band", "field"),
        check_vma=False,
    )
```
